512 devices in a mesh: xt: 32 (over z_lo, x, core), yt: 16 (over z_hi, y).
Axes of the slice: x: 4, y: 4, z: 16 (z_hi: 4, z_lo: 4; z = z_hi * 4 + z_lo), core: 2. Of those that a mesh axis runs over, the one named last changes fastest.
Arguments:
- cotangent: bfloat16 [512, 512, 1024], P('xt', 'yt'), may hold values from -6 to 6
- preact: bfloat16 [512, 512, 1024], P('xt', 'yt'), may hold values from -8 to 8
- spectra: float32 [32, 32, 512], P('xt', 'yt'), may hold values from -6 to 6
- spectral_weight: float32 [32, 32, 8192], P('xt', 'yt'), may hold values from -12 to 12
- local_weight: bfloat16 [16, 16], replicated, may hold values from -1.5 to 1.5
Outputs:
- grad_input: float32 [512, 512, 1024], P('xt', 'yt')
- grad_weight: float32 [32, 32, 8192], P('xt', 'yt')
The draws below stay inside these ranges and needn't reach their ends.
All inputs are finite; a program needn't handle non-finite values.
Results may differ from the reference program's by a relative error of at most 0.0034.
Values may be sent and summed in bfloat16 or wider, within the bound.
No kernel may reach another device: no remote copies, remote signals or barrier semaphores. Data moves between devices by JAX's collectives and lax.ppermute only.
A program may use at most 64 MiB of HBM per device.

```python
import math
import jax
import jax.numpy as jnp
from jax import lax

C = 16
MX = 32
MY = 32
MZ = 16
NZ = 64
CX = 16
NX = 512
NY = 512
N_XT = 32


def levels(stream_key, extent, pieces, least, high):
    level = 1.0
    for axis_at, shards_of in pieces:
        draws = jax.random.uniform(jax.random.fold_in(jax.random.fold_in(stream_key, 6), axis_at), (shards_of,), jnp.float32, least / len(pieces), high / len(pieces))
        level = level * jnp.repeat(jnp.exp(draws), extent[axis_at] // shards_of).reshape((-1,) + (1,) * (len(extent) - 1 - axis_at))
    return level


def centred(key, extent, width, bound, shards=(), held_as=jnp.bfloat16):
    values = jax.random.normal(key, extent, jnp.float32) * width
    if len(shards) > 0:
        values = levels(key, extent, shards, -0.22, 0.18) * values
    return jnp.clip(values, min=-bound, max=bound).astype(held_as)


def setup_inputs(seed: int = 0) -> dict:
    key_list = jax.random.split(jax.random.key(seed), 6)
    return {
        "cotangent": centred(key_list[0], (NX, NY, NZ * C), 1.0, 6.0, ((0, 32), (1, 16))),
        "preact": centred(key_list[1], (NX, NY, NZ * C), 1.5, 8.0, ((0, 32), (1, 16))),
        "spectra": centred(key_list[2], (MX, MY, 2 * MZ * C), 1.0, 6.0, ((0, 32), (1, 16)), jnp.float32),
        "spectral_weight": centred(key_list[3], (MX, MY, 2 * MZ * C * C), 2.0, 12.0, ((0, 32), (1, 16)), jnp.float32),
        "local_weight": centred(key_list[4], (C, C), C ** -0.5, 1.5),
    }


PRECISE = lax.Precision.HIGHEST

def mode_ids(mode_count, length):
    ordinal = jnp.arange(mode_count, dtype=jnp.int32)
    return jnp.where(ordinal < mode_count // 2, ordinal, ordinal + (length - mode_count)).astype(jnp.int32)

def phase_pair(positions, mode_list, length):
    product = positions[:, None] * mode_list[None, :] % length
    phase_angle = product.astype(jnp.float32) * (2.0 * math.pi / length)
    return (jnp.cos(phase_angle), jnp.sin(phase_angle))

def gelu_slope(pre_value):
    normal_cdf = 0.5 * (1.0 + jax.scipy.special.erf(pre_value * (1.0 / math.sqrt(2.0))))
    return normal_cdf + pre_value * jnp.exp(-0.5 * pre_value * pre_value) * (1.0 / math.sqrt(2.0 * math.pi))

def slope_grad(cotangent, preact):
    pre_value = preact.astype(jnp.float32)
    return (cotangent.astype(jnp.float32) * gelu_slope(pre_value)).astype(jnp.bfloat16)

def rotate_sum(data, cosine_table, sine_table, form, direction):
    half_width = data.shape[-1] // 2
    real_part = data[..., :half_width]
    imaginary = data[..., half_width:]

    def contract(operand, factor):
        return jnp.einsum(form, operand, factor, precision=PRECISE)
    new_real = contract(real_part, cosine_table) - direction * contract(imaginary, sine_table)
    new_imaginary = contract(imaginary, cosine_table) + direction * contract(real_part, sine_table)
    return jnp.concatenate([new_real, new_imaginary], axis=-1)

def forward_depth(grid_depth, mode_count):
    cosine_table, sine_table = phase_pair(jnp.arange(grid_depth, dtype=jnp.int32), jnp.arange(mode_count, dtype=jnp.int32), grid_depth)
    weighting = jnp.where(jnp.arange(mode_count) == 0, 1.0, 2.0).astype(jnp.float32)
    return jnp.stack([cosine_table * weighting, -sine_table * weighting], axis=1).astype(jnp.bfloat16)

def inverse_depth(grid_depth, mode_count):
    cosine_table, sine_table = phase_pair(jnp.arange(grid_depth, dtype=jnp.int32), jnp.arange(mode_count, dtype=jnp.int32), grid_depth)
    return jnp.stack([cosine_table.T, -sine_table.T], axis=0)

def depth_project(grad_pre, factor_table, channels):
    tile_rows, tile_columns, row_width = grad_pre.shape
    grid_depth = row_width // channels
    grid_cells = grad_pre.reshape(tile_rows, tile_columns, grid_depth, channels)
    result = jnp.einsum('xyzc,zrk->xyrkc', grid_cells.astype(jnp.float32), factor_table.astype(jnp.float32), precision=PRECISE)
    return result.reshape(tile_rows, tile_columns, -1)

def depth_expand(data, factor_table, channels):
    tile_rows, tile_columns, row_width = data.shape
    mode_count = factor_table.shape[1]
    mode_cells = data.reshape(tile_rows, tile_columns, 2, mode_count, channels)
    result = jnp.einsum('xyrkc,rkz->xyzc', mode_cells, factor_table, precision=PRECISE)
    return result.reshape(tile_rows, tile_columns, -1)

def mode_update(mode_grad, spectra, spectral_weight, mode_count, channels):
    lead_first, lead_second = (mode_grad.shape[0], mode_grad.shape[1])
    gradient = mode_grad.reshape(lead_first, lead_second, 2, mode_count, channels)
    saved = spectra.reshape(lead_first, lead_second, 2, mode_count, channels)
    weights = spectral_weight.reshape(lead_first, lead_second, 2, mode_count, channels, channels)
    grad_real, grad_imaginary = (gradient[:, :, 0], gradient[:, :, 1])
    saved_real, saved_imaginary = (saved[:, :, 0], saved[:, :, 1])
    weight_real, weight_imaginary = (weights[:, :, 0], weights[:, :, 1])
    outer_real = saved_real[..., :, None] * grad_real[..., None, :] + saved_imaginary[..., :, None] * grad_imaginary[..., None, :]
    outer_imaginary = saved_real[..., :, None] * grad_imaginary[..., None, :] - saved_imaginary[..., :, None] * grad_real[..., None, :]
    grad_weight = jnp.stack([outer_real, outer_imaginary], axis=2).reshape(lead_first, lead_second, -1)

    def contract(matrix, vector):
        return jnp.einsum('abkco,abko->abkc', matrix, vector, precision=PRECISE)
    back_real = contract(weight_real, grad_real) + contract(weight_imaginary, grad_imaginary)
    back_imaginary = contract(weight_real, grad_imaginary) - contract(weight_imaginary, grad_real)
    spectra_grad = jnp.stack([back_real, back_imaginary], axis=2).reshape(lead_first, lead_second, -1).astype(jnp.bfloat16)
    return (grad_weight, spectra_grad)

def reference(cotangent, preact, spectra, spectral_weight, local_weight):
    norm_factor = 1.0 / math.sqrt(NX * NY * NZ)
    cosine_first, sine_first = phase_pair(jnp.arange(NX, dtype=jnp.int32), mode_ids(MX, NX), NX)
    cosine_second, sine_second = phase_pair(jnp.arange(NY, dtype=jnp.int32), mode_ids(MY, NY), NY)
    depth_forward = forward_depth(NZ, MZ)
    depth_inverse = inverse_depth(NZ, MZ)
    starts = jnp.arange(N_XT, dtype=jnp.int32) * CX

    def forward_block(first_row):
        cotangent_rows = lax.dynamic_slice_in_dim(cotangent, first_row.astype(jnp.int32), CX, 0)
        preact_rows = lax.dynamic_slice_in_dim(preact, first_row.astype(jnp.int32), CX, 0)
        grad_pre = slope_grad(cotangent_rows, preact_rows)
        depth_data = depth_project(grad_pre, depth_forward, C)
        return rotate_sum(depth_data, cosine_second, sine_second, 'xyf,yj->xjf', -1.0)
    after_second = lax.map(forward_block, starts).reshape(NX, MY, -1)
    mode_grad = rotate_sum(after_second, cosine_first, sine_first, 'xjf,xi->ijf', -1.0) * norm_factor
    grad_weight, spectra_grad = mode_update(mode_grad, spectra, spectral_weight, MZ, C)
    expanded_first = rotate_sum(spectra_grad.astype(jnp.float32), cosine_first, sine_first, 'ijf,xi->xjf', 1.0)

    def inverse_block(first_row):
        cotangent_rows = lax.dynamic_slice_in_dim(cotangent, first_row.astype(jnp.int32), CX, 0)
        preact_rows = lax.dynamic_slice_in_dim(preact, first_row.astype(jnp.int32), CX, 0)
        grad_pre = slope_grad(cotangent_rows, preact_rows)
        block_modes = lax.dynamic_slice_in_dim(expanded_first, first_row.astype(jnp.int32), CX, 0)
        expanded_second = rotate_sum(block_modes, cosine_second, sine_second, 'xjf,yj->xyf', 1.0)
        spectral_part = depth_expand(expanded_second, depth_inverse, C) * norm_factor
        grid_cells = grad_pre.reshape(CX, NY, NZ, C).astype(jnp.float32)
        local_part = jnp.einsum('xyzo,co->xyzc', grid_cells, local_weight.astype(jnp.float32), precision=PRECISE)
        return spectral_part + local_part.reshape(CX, NY, -1)
    grad_input = lax.map(inverse_block, starts).reshape(NX, NY, -1)
    return (grad_input, grad_weight)
```

```python
import functools
import math

import jax
import jax.numpy as jnp
import ml_dtypes
import numpy as np
from jax import lax
from jax.experimental import pallas as pl
from jax.experimental.pallas import tpu as pltpu
from jax.sharding import Mesh
from jax.sharding import PartitionSpec as P

TILE_X, TILE_Y, DEPTH, CH = 16, 32, 64, 16
KX, KY, KZ = 32, 32, 16
NX, NY = 512, 512
ZL, XS, CS, ZH, YS = 4, 4, 2, 4, 4
ROW = DEPTH * CH
HALF = KZ * CH
STEPS = 4
STEP_X = TILE_X // STEPS
STEP_ROWS = STEP_X * TILE_Y
F32, BF16 = jnp.float32, jnp.bfloat16
MIB = 1024 * 1024


def split_table(table):
    high = table.astype(ml_dtypes.bfloat16)
    low = (table - high.astype(np.float64)).astype(ml_dtypes.bfloat16)
    return high, low


def mode_ids(count, length):
    ordinal = np.arange(count)
    return np.where(ordinal < count // 2, ordinal, ordinal + length - count)


def phase(positions, modes, length):
    angle = (np.outer(modes, positions) % length) * (2.0 * np.pi / length)
    return np.cos(angle), np.sin(angle)


KX_ORDER = np.array([zl * 8 + x * 2 + c for x in range(XS) for c in range(CS) for zl in range(ZL)])


def place_of(ky):
    return ky // 8, ky % 8 // 2, ky % 2


@functools.cache
def tables():
    ky = mode_ids(KY, NY)
    kx = mode_ids(KX, NX)[KX_ORDER]
    forward_y, inverse_y, forward_x, inverse_x = [], [], [], []
    for tile in range(NY // TILE_Y):
        cosine, sine = phase(tile * TILE_Y + np.arange(TILE_Y), ky, NY)
        rows = np.stack(
            [np.concatenate([cosine, sine], 1), np.concatenate([-sine, cosine], 1)], 1
        ).reshape(2 * KY, 2 * TILE_Y)
        high, low = split_table(rows)
        forward_y.append(np.concatenate([high, high, low], 1))
        rows = np.concatenate(
            [np.concatenate([cosine.T, -sine.T], 1), np.concatenate([sine.T, cosine.T], 1)], 0
        )
        high, low = split_table(rows)
        inverse_y.append(np.concatenate([high, high, low], 1))
    for tile in range(NX // TILE_X):
        cosine, sine = phase(tile * TILE_X + np.arange(TILE_X), kx, NX)
        rows = np.concatenate(
            [np.concatenate([cosine, sine], 1), np.concatenate([-sine, cosine], 1)], 0
        )
        high, low = split_table(rows)
        forward_x.append(np.concatenate([high, high, low], 1))
        rows = np.concatenate(
            [np.concatenate([cosine.T, -sine.T], 1), np.concatenate([sine.T, cosine.T], 1)], 0
        )
        high, low = split_table(rows)
        inverse_x.append(np.concatenate([high, low], 1))
    depth_angle = (np.outer(np.arange(DEPTH), np.arange(KZ)) % DEPTH) * (2.0 * np.pi / DEPTH)
    weight = np.where(np.arange(KZ) == 0, 1.0, 2.0)
    factor = np.stack([np.cos(depth_angle) * weight, -np.sin(depth_angle) * weight], 1)
    factor = factor.astype(np.float32).astype(ml_dtypes.bfloat16).astype(np.float64)
    eye = np.eye(CH)
    project = np.kron(factor.reshape(DEPTH, 2 * KZ), eye).astype(ml_dtypes.bfloat16)
    expand = np.stack([np.cos(depth_angle).T, -np.sin(depth_angle).T], 0)
    expand = np.kron(expand.reshape(2 * KZ, DEPTH), eye) / math.sqrt(NX * NY * DEPTH)
    expand_high, expand_low = split_table(expand)
    kz8, ones = np.eye(8), np.ones((1, CH))
    spread_o = np.kron(kz8, np.kron(ones, eye)).astype(ml_dtypes.bfloat16)
    spread_c = np.kron(kz8, np.kron(eye, ones)).astype(ml_dtypes.bfloat16)
    return dict(
        forward_y=np.stack(forward_y),
        inverse_y=np.stack(inverse_y),
        forward_x=np.stack(forward_x),
        inverse_x=np.stack(inverse_x),
        project=project,
        expand_high=expand_high,
        expand_low=expand_low,
        spread_o=spread_o,
        spread_c=spread_c,
    )


def dot(left, right):
    return lax.dot_general(left, right, (((1,), (0,)), ((), ())), preferred_element_type=F32)


def split(value):
    high = value.astype(BF16)
    return high, (value - high.astype(F32)).astype(BF16)


def split_rows(value):
    high, low = split(value)
    return jnp.concatenate([high, low, high], 0)


def three_parts(value):
    high = value.astype(BF16)
    rest = value - high.astype(F32)
    middle = rest.astype(BF16)
    low = (rest - middle.astype(F32)).astype(BF16)
    return jnp.concatenate([high, middle, low], 0)


def sum_parts(value):
    rows = value.shape[0] // 3
    return value[:rows] + (value[rows : 2 * rows] + value[2 * rows :])


def gelu_slope(pre_value):
    normal_cdf = 0.5 * (1.0 + lax.erf(pre_value * (1.0 / math.sqrt(2.0))))
    return normal_cdf + pre_value * jnp.exp(-0.5 * pre_value * pre_value) * (
        1.0 / math.sqrt(2.0 * math.pi)
    )


def mode_rows(ky, quarter):
    zh, y, local = place_of(ky)
    return pl.ds(y * 1024 + zh * 8 + quarter * 2 + local, KX, stride=32)


def project_kernel(
    at_ref, cot_ref, pre_ref, project_ref, fy_ref, fx_ref, slope_ref, out_ref, t_refs, p_ref
):
    step = pl.program_id(0)
    pre_value = pre_ref[...].astype(F32)
    slope = (cot_ref[...].astype(F32) * gelu_slope(pre_value)).astype(BF16)
    slope_ref[...] = slope
    depth = dot(slope, project_ref[...])
    for local in range(STEP_X):
        block = depth[local * TILE_Y : (local + 1) * TILE_Y]
        stacked = jnp.concatenate([block[:, :HALF], block[:, HALF:]], 0)
        turned = dot(fy_ref[...], split_rows(stacked))
        for half in range(2):
            t_refs[half, pl.ds(step * STEP_X + local, 2 * KY, stride=TILE_X), :] = turned[
                :, half * 128 : (half + 1) * 128
            ]

    @pl.when(step == STEPS - 1)
    def _():
        for ky in range(KY):
            rows = slice(ky * 2 * TILE_X, (ky + 1) * 2 * TILE_X)
            stacked = jnp.concatenate([t_refs[0, rows, :], t_refs[1, rows, :]], 1)
            turned = dot(fx_ref[...], split_rows(stacked))
            for part in range(2):
                for half in range(2):
                    p_ref[mode_rows(ky, part * 2 + half), :] = turned[
                        part * KX : (part + 1) * KX, half * 128 : (half + 1) * 128
                    ]
        out_ref[...] = p_ref[...].astype(BF16)


def project_call(place, cotangent, preact, table):
    def whole(shape):
        return pl.BlockSpec(shape, lambda i, at: (0, 0))

    rows = TILE_X * TILE_Y
    chunk = pl.BlockSpec((STEP_ROWS, ROW), lambda i, at: (i, 0))
    return pl.pallas_call(
        project_kernel,
        grid_spec=pltpu.PrefetchScalarGridSpec(
            num_scalar_prefetch=1,
            grid=(STEPS,),
            in_specs=[
                chunk,
                chunk,
                whole((ROW, 2 * HALF)),
                pl.BlockSpec((None, 2 * KY, 6 * TILE_Y), lambda i, at: (at[1], 0, 0)),
                pl.BlockSpec((None, 2 * KX, 6 * TILE_X), lambda i, at: (at[0], 0, 0)),
            ],
            out_specs=[chunk, whole((4096, 128))],
            scratch_shapes=[
                pltpu.VMEM((2, 2 * KY * TILE_X, 128), F32),
                pltpu.VMEM((4096, 128), F32),
            ],
        ),
        out_shape=[
            jax.ShapeDtypeStruct((rows, ROW), BF16),
            jax.ShapeDtypeStruct((4096, 128), BF16),
        ],
        compiler_params=pltpu.CompilerParams(vmem_limit_bytes=24 * MIB),
        name="project",
    )(place, cotangent, preact, table["project"], table["forward_y"], table["forward_x"])


def update_kernel(sum_ref, spectra_ref, weight_ref, spread_o_ref, spread_c_ref, gw_ref, sg_ref):
    norm = 1.0 / math.sqrt(NX * NY * DEPTH)
    grad = jnp.sum(sum_ref[...], 0) * norm
    saved = jnp.concatenate([spectra_ref[:, b * 128 : (b + 1) * 128] for b in range(4)], 0)
    weight = jnp.concatenate([weight_ref[:, b * 2048 : (b + 1) * 2048] for b in range(4)], 0)
    grad_wide = sum_parts(dot(three_parts(grad), spread_o_ref[...]))
    saved_wide = sum_parts(dot(three_parts(saved), spread_c_ref[...]))

    def combine(value):
        real, imaginary = value[:4], value[4:]
        grad_real, grad_imaginary = grad_wide[:4], grad_wide[4:]
        return jnp.concatenate(
            [
                real * grad_real + imaginary * grad_imaginary,
                real * grad_imaginary - imaginary * grad_real,
            ],
            0,
        )

    outer = combine(saved_wide)
    for b in range(4):
        gw_ref[:, b * 2048 : (b + 1) * 2048] = outer[2 * b : 2 * b + 2]
    back = lax.dot_general(
        three_parts(combine(weight)),
        spread_c_ref[...],
        (((1,), (1,)), ((), ())),
        preferred_element_type=F32,
    )
    back = sum_parts(back)
    sg_ref[...] = jnp.broadcast_to(back[None], sg_ref.shape).astype(sg_ref.dtype)


def update_call(sums, spectra, weight, table):
    return pl.pallas_call(
        update_kernel,
        out_shape=[
            jax.ShapeDtypeStruct((2, 8192), F32),
            jax.ShapeDtypeStruct((ZL * ZH, 8, 128), BF16),
        ],
        compiler_params=pltpu.CompilerParams(vmem_limit_bytes=16 * MIB),
        name="update",
    )(sums, spectra, weight, table["spread_o"], table["spread_c"])


def expand_kernel(
    at_ref,
    modes_ref,
    slope_ref,
    local_ref,
    high_ref,
    low_ref,
    iy_ref,
    ix_ref,
    out_ref,
    m_ref,
    e_refs,
    l_ref,
):
    step = pl.program_id(0)

    @pl.when(step == 0)
    def _():
        m_ref[...] = modes_ref[...].astype(F32)
        for ky in range(KY):
            parts = [
                jnp.concatenate(
                    [m_ref[mode_rows(ky, part * 2 + half), :] for half in range(2)], 1
                )
                for part in range(2)
            ]
            stacked = jnp.concatenate(parts, 0).astype(BF16)
            turned = dot(ix_ref[...], jnp.concatenate([stacked, stacked], 0))
            rows = slice(ky * 2 * TILE_X, (ky + 1) * 2 * TILE_X)
            for half in range(2):
                e_refs[half, rows, :] = turned[:, half * 128 : (half + 1) * 128]
        shape = (16 * CH, CH)
        pick = lax.broadcasted_iota(jnp.int32, shape, 0) % CH
        pick = (pick == lax.broadcasted_iota(jnp.int32, shape, 1)).astype(F32).astype(BF16)
        rows = lax.dot_general(
            pick, local_ref[...], (((1,), (1,)), ((), ())), preferred_element_type=F32
        ).astype(BF16)
        full = lax.dot_general(
            rows, pick, (((1,), (1,)), ((), ())), preferred_element_type=F32
        )
        shape = (16 * CH, 16 * CH)
        same = (
            lax.broadcasted_iota(jnp.int32, shape, 0) // CH
            == lax.broadcasted_iota(jnp.int32, shape, 1) // CH
        )
        l_ref[...] = jnp.where(same, full, 0.0).astype(BF16)

    cells = []
    for local in range(STEP_X):
        at = step * STEP_X + local
        parts = [
            jnp.concatenate(
                [
                    e_refs[half, pl.ds(part * TILE_X + at, KY, stride=2 * TILE_X), :]
                    for half in range(2)
                ],
                1,
            )
            for part in range(2)
        ]
        turned = dot(iy_ref[...], split_rows(jnp.concatenate(parts, 0)))
        cells.append(jnp.concatenate([turned[:TILE_Y], turned[TILE_Y:]], 1))
    high, low = split(jnp.concatenate(cells, 0))
    total = dot(high, high_ref[...]) + dot(low, high_ref[...]) + dot(high, low_ref[...])
    slope = slope_ref[...]
    for part in range(4):
        lanes = slice(part * 256, (part + 1) * 256)
        out_ref[:, lanes] = total[:, lanes] + dot(slope[:, lanes], l_ref[...])


def expand_call(place, modes, slope, local_weight, table):
    def whole(shape):
        return pl.BlockSpec(shape, lambda i, at: (0, 0))

    rows = TILE_X * TILE_Y
    chunk = pl.BlockSpec((STEP_ROWS, ROW), lambda i, at: (i, 0))
    return pl.pallas_call(
        expand_kernel,
        grid_spec=pltpu.PrefetchScalarGridSpec(
            num_scalar_prefetch=1,
            grid=(STEPS,),
            in_specs=[
                whole((4096, 128)),
                chunk,
                whole((CH, CH)),
                whole((2 * HALF, ROW)),
                whole((2 * HALF, ROW)),
                pl.BlockSpec((None, 2 * TILE_Y, 6 * KY), lambda i, at: (at[1], 0, 0)),
                pl.BlockSpec((None, 2 * TILE_X, 4 * KX), lambda i, at: (at[0], 0, 0)),
            ],
            out_specs=chunk,
            scratch_shapes=[
                pltpu.VMEM((4096, 128), F32),
                pltpu.VMEM((2, 2 * KY * TILE_X, 128), F32),
                pltpu.VMEM((16 * CH, 16 * CH), BF16),
            ],
        ),
        out_shape=jax.ShapeDtypeStruct((rows, ROW), F32),
        compiler_params=pltpu.CompilerParams(vmem_limit_bytes=24 * MIB),
        name="expand",
    )(
        place,
        modes,
        slope,
        local_weight,
        table["expand_high"],
        table["expand_low"],
        table["inverse_y"],
        table["inverse_x"],
    )


PLANE = ("y", "x", "c")
LINE = ("zl", "zh")


def on_device(cotangent, preact, spectra, spectral_weight, local_weight):
    table = {name: jnp.asarray(value) for name, value in tables().items()}
    place = jnp.stack([lax.axis_index(("zl", "x", "c")), lax.axis_index(("zh", "y"))])
    place = place.astype(jnp.int32)
    rows = TILE_X * TILE_Y
    slope, partial = project_call(
        place, cotangent.reshape(rows, ROW), preact.reshape(rows, ROW), table
    )
    partial = lax.all_to_all(partial.reshape(32, 128, 128), PLANE, 0, 0, tiled=True)
    sums = jnp.sum(partial.astype(F32), 0).reshape(ZL * ZH, 8, 128)
    sums = lax.all_to_all(sums, LINE, 0, 0, tiled=True)
    grad_weight, back = update_call(
        sums, spectra.reshape(2, 2 * HALF), spectral_weight.reshape(2, 8192), table
    )
    back = lax.all_to_all(back, LINE, 0, 0, tiled=True)
    back = jnp.broadcast_to(back.reshape(1, 128, 128), (32, 128, 128))
    modes = lax.all_to_all(back, PLANE, 0, 0, tiled=True)
    result = expand_call(place, modes.reshape(4096, 128), slope, local_weight, table)
    return result.reshape(TILE_X, TILE_Y, ROW), grad_weight.reshape(1, 2, 8192)


def solution(mesh):
    fine = Mesh(mesh.devices.reshape(ZL, XS, CS, ZH, YS), ("zl", "x", "c", "zh", "y"))
    split_spec = P(("zl", "x", "c"), ("zh", "y"), None)
    return jax.shard_map(
        on_device,
        mesh=fine,
        in_specs=(split_spec, split_spec, split_spec, split_spec, P()),
        out_specs=(split_spec, split_spec),
        check_vma=False,
    )
```

```python
import functools
import math

import jax
import jax.numpy as jnp
import ml_dtypes
import numpy as np
from jax import lax
from jax.experimental import pallas as pl
from jax.experimental.pallas import tpu as pltpu
from jax.sharding import Mesh
from jax.sharding import PartitionSpec as P

TILE_X, TILE_Y, DEPTH, CH = 16, 32, 64, 16
KX, KY, KZ = 32, 32, 16
NX, NY = 512, 512
ZL, XS, CS, ZH, YS = 4, 4, 2, 4, 4
ROW = DEPTH * CH
HALF = KZ * CH
QUARTER = 128
ROWS = TILE_X * TILE_Y
CHUNKS = 8
CHUNK_ROWS = ROWS // CHUNKS
NORM = 1.0 / math.sqrt(NX * NY * DEPTH)
F32, BF16 = jnp.float32, jnp.bfloat16
MIB = 1024 * 1024
PLANE = ("y", "x")
LINE = ("zl", "zh", "c")


def split_table(table):
    high = table.astype(ml_dtypes.bfloat16)
    low = (table - high.astype(np.float64)).astype(ml_dtypes.bfloat16)
    return high, low


def mode_ids(count, length):
    ordinal = np.arange(count)
    return np.where(ordinal < count // 2, ordinal, ordinal + length - count)


def phase(positions, modes, length):
    angle = (np.outer(modes, positions) % length) * (2.0 * np.pi / length)
    return np.cos(angle), np.sin(angle)


KX_ORDER = np.array([zl * 8 + x * 2 + c for x in range(XS) for zl in range(ZL) for c in range(CS)])
KY_ORDER = np.array([zh * 8 + y * 2 + k for y in range(YS) for zh in range(ZH) for k in range(2)])


def rotation(cosine, sine):
    return np.stack([np.stack([cosine, sine]), np.stack([-sine, cosine])])


@functools.cache
def tables():
    ky = mode_ids(KY, NY)[KY_ORDER]
    kx = mode_ids(KX, NX)[KX_ORDER]
    forward_y, inverse_y, forward_x = [], [], []
    for tile in range(NY // TILE_Y):
        turn = rotation(*phase(tile * TILE_Y + np.arange(TILE_Y), ky, NY))
        turn = turn.reshape(2, 2, YS, 8, TILE_Y)
        rows = turn.transpose(2, 0, 3, 1, 4).reshape(2 * KY, 2 * TILE_Y)
        high, low = split_table(rows)
        forward_y.append(np.concatenate([high, high, low], 1))
        high, low = split_table(rows.reshape(2 * KY, 2, TILE_Y).transpose(1, 2, 0).reshape(2 * TILE_Y, -1))
        inverse_y.append(np.concatenate([high, high, low], 1))
    for tile in range(NX // TILE_X):
        parts = []
        for source in (tile, tile ^ 1):
            turn = rotation(*phase(source * TILE_X + np.arange(TILE_X), kx, NX))
            parts.append(turn.transpose(2, 0, 3, 1).reshape(2 * KX, 2 * TILE_X))
        forward_x.append(np.concatenate(split_table(np.concatenate(parts, 1)), 1))
    depth_angle = (np.outer(np.arange(DEPTH), np.arange(KZ)) % DEPTH) * (2.0 * np.pi / DEPTH)
    weight = np.where(np.arange(KZ) == 0, 1.0, 2.0)
    factor = np.stack([np.cos(depth_angle) * weight, -np.sin(depth_angle) * weight], 1)
    factor = factor.astype(np.float32).astype(ml_dtypes.bfloat16).astype(np.float32)
    project = np.repeat(factor.reshape(DEPTH, 2, 2, 8).transpose(2, 0, 1, 3), CH, 3)
    project = project.reshape(2, DEPTH, HALF).astype(ml_dtypes.bfloat16)
    expand = np.stack([np.cos(depth_angle).T, -np.sin(depth_angle).T], 0) * NORM
    expand = expand.reshape(2, 2, 8, DEPTH).transpose(1, 0, 2, 3).reshape(2, KZ, DEPTH)
    expand = np.stack([np.kron(part, np.eye(CH)) for part in expand])
    expand_high, expand_low = split_table(expand)
    eye, kz8, ones = np.eye(CH), np.eye(8), np.ones((1, CH))
    spread_o = np.kron(kz8, np.kron(ones, eye)).astype(ml_dtypes.bfloat16)
    spread_c = np.kron(kz8, np.kron(eye, ones)).astype(ml_dtypes.bfloat16)
    return dict(
        forward_y=np.stack(forward_y),
        inverse_y=np.stack(inverse_y),
        forward_x=np.stack(forward_x),
        project=project,
        expand_high=expand_high,
        expand_low=expand_low,
        spread_o=spread_o,
        spread_c=spread_c,
    )


def dot(left, right):
    return lax.dot_general(left, right, (((1,), (0,)), ((), ())), preferred_element_type=F32)


def dot_last(left, right):
    return lax.dot_general(left, right, (((1,), (1,)), ((), ())), preferred_element_type=F32)


def split(value):
    high = value.astype(BF16)
    return high, (value - high.astype(F32)).astype(BF16)


def store_split(ref, lanes, value):
    rows = value.shape[0]
    high, low = split(value)
    ref[:rows, lanes] = high
    ref[rows : 2 * rows, lanes] = low
    ref[2 * rows :, lanes] = high


def three_parts(value):
    high = value.astype(BF16)
    rest = value - high.astype(F32)
    middle = rest.astype(BF16)
    low = (rest - middle.astype(F32)).astype(BF16)
    return jnp.concatenate([high, middle, low], 0)


def sum_parts(value):
    rows = value.shape[0] // 3
    return value[:rows] + (value[rows : 2 * rows] + value[2 * rows :])


def gelu_slope(pre_value):
    normal_cdf = 0.5 * (1.0 + lax.erf(pre_value * (1.0 / math.sqrt(2.0))))
    return normal_cdf + pre_value * jnp.exp(-0.5 * pre_value * pre_value) * (
        1.0 / math.sqrt(2.0 * math.pi)
    )


def lanes_of(at):
    return slice(at * QUARTER, (at + 1) * QUARTER)


def iota(shape, axis):
    return lax.broadcasted_iota(jnp.int32, shape, axis)


def one_hot(condition):
    return condition.astype(F32).astype(BF16)


BLOCK, CELLS = 512, 256


def fill_forward(out_ref, small):
    shape = (128, 1024)
    cells = one_hot(iota(shape, 1) >> 3 == iota(shape, 0))
    shape = (128, 64)
    twice = one_hot(iota(shape, 0) >> 1 == iota(shape, 1))
    wide = dot(twice, dot(small, cells).astype(BF16))
    shape = (8, CELLS)
    local, ky = iota(shape, 0) & 1, iota(shape, 1) & 7
    masks = [(ky == 2 * zh + local).astype(F32) for zh in range(ZH)]
    for part in range(2):
        for source in range(2):
            first = (part * 2 + source) * CELLS
            for group in range(16):
                rows = wide[group * 8 : (group + 1) * 8, first : first + CELLS]
                rows = jnp.concatenate([rows * mask for mask in masks], 0).astype(BF16)
                out_ref[source, part, group * 32 : (group + 1) * 32, :] = rows


def fill_inverse(out_ref, small):
    shape = (64, BLOCK)
    row, column = iota(shape, 0), iota(shape, 1)
    modes = one_hot((column >> 5) * 4 + (column >> 1 & 3) == row)
    wide = lax.dot_general(small, modes, (((0,), (0,)), ((), ())), preferred_element_type=F32)
    shape = (8, BLOCK)
    row, column = iota(shape, 0), iota(shape, 1)
    mask = ((column >> 3 & 3) * 2 + (column & 1) == row).astype(F32)
    for part in range(2):
        for cell in range(TILE_X):
            at = part * 64 + cell * 2
            rows = [jnp.broadcast_to(wide[i : i + 1], shape) * mask for i in (at, at + 1)]
            out_ref[part, cell * 16 : (cell + 1) * 16, :] = jnp.concatenate(rows, 0).astype(BF16)


def fill_local(out_ref, local_ref):
    shape = (16 * CH, CH)
    pick = one_hot((iota(shape, 0) & (CH - 1)) == iota(shape, 1))
    full = dot_last(dot_last(pick, local_ref[...]).astype(BF16), pick)
    shape = (16 * CH, 16 * CH)
    same = iota(shape, 0) >> 4 == iota(shape, 1) >> 4
    out_ref[...] = jnp.where(same, full, 0.0).astype(BF16)


def fill_project(f_ref, table_ref, half):
    shape = (CH, HALF)
    same = iota(shape, 0) == (iota(shape, 1) & (CH - 1))
    table = table_ref[half].astype(F32)
    for z in range(DEPTH):
        factor = jnp.broadcast_to(table[z : z + 1], shape)
        f_ref[z * CH : (z + 1) * CH, :] = jnp.where(same, factor, 0.0).astype(BF16)


def slope_kernel(
    at_ref,
    cot_hbm,
    pre_hbm,
    local_hbm,
    table_hbm,
    fx_hbm,
    fy_hbm,
    iy_hbm,
    slope_ref,
    send_ref,
    own_ref,
    forward_ref,
    inverse_ref,
    l_ref,
    fy_ref,
    iy_ref,
    cot_ref,
    pre_ref,
    local_ref,
    table_ref,
    fx_ref,
    f_ref,
    sems,
    small_sems,
):
    def copies(chunk):
        rows = pl.ds(chunk * CHUNK_ROWS, CHUNK_ROWS)
        return (
            pltpu.make_async_copy(cot_hbm.at[rows], cot_ref.at[rows], sems.at[0, chunk]),
            pltpu.make_async_copy(pre_hbm.at[rows], pre_ref.at[rows], sems.at[1, chunk]),
        )

    small = [
        pltpu.make_async_copy(source, target, small_sems.at[i])
        for i, (source, target) in enumerate(
            (
                (fx_hbm.at[at_ref[0]], fx_ref),
                (table_hbm, table_ref),
                (local_hbm, local_ref),
                (fy_hbm.at[at_ref[1]], fy_ref),
                (iy_hbm.at[at_ref[1]], iy_ref),
            )
        )
    ]
    for copy in small:
        copy.start()
    for chunk in range(CHUNKS):
        for copy in copies(chunk):
            copy.start()
    for copy in small:
        copy.wait()
    fill_project(f_ref, table_ref, 1 - at_ref[2])
    fill_project(own_ref, table_ref, at_ref[2])
    fill_forward(forward_ref, fx_ref[...])
    fill_inverse(inverse_ref, fx_ref[...])
    fill_local(l_ref, local_ref)
    for chunk in range(CHUNKS):
        for copy in copies(chunk):
            copy.wait()
        rows = slice(chunk * CHUNK_ROWS, (chunk + 1) * CHUNK_ROWS)
        pre_value = pre_ref[rows, :].astype(F32)
        slope = (cot_ref[rows, :].astype(F32) * gelu_slope(pre_value)).astype(BF16)
        slope_ref[rows, :] = slope
        if (chunk + 1) * 2 % CHUNKS == 0:
            rows = slice((chunk + 1) * CHUNK_ROWS - ROWS // 2, (chunk + 1) * CHUNK_ROWS)
            send_ref[rows, :] = dot(slope_ref[rows, :], f_ref[...])


def turn_y(depth, fy_ref, rhs_ref, high_ref, low_ref):
    for x in range(TILE_X):
        block = depth[x * TILE_Y : (x + 1) * TILE_Y]
        stacked = jnp.concatenate([block[:, :QUARTER], block[:, QUARTER:]], 0)
        store_split(rhs_ref, lanes_of(x), stacked)
    turned = dot(fy_ref[...], rhs_ref[...])
    for x in range(TILE_X):
        for y in range(YS):
            high, low = split(turned[y * 16 : (y + 1) * 16, lanes_of(x)])
            high_ref[x * 16 : (x + 1) * 16, lanes_of(y)] = high
            low_ref[x * 16 : (x + 1) * 16, lanes_of(y)] = low


def turn_x(table_high, table_low, high, low):
    return dot(table_high, high) + dot(table_high, low) + dot(table_low, high)


def own_kernel(slope_ref, f_ref, x_ref, fy_ref, part_ref, rhs_ref, high_ref, low_ref):
    turn_y(dot(slope_ref[...], f_ref[...]), fy_ref, rhs_ref, high_ref, low_ref)
    part_ref[...] = turn_x(x_ref[0, 0], x_ref[0, 1], high_ref[...], low_ref[...])


def modes_kernel(depth_ref, part_ref, x_ref, fy_ref, out_ref, rhs_ref, high_ref, low_ref):
    turn_y(depth_ref[...], fy_ref, rhs_ref, high_ref, low_ref)
    turned = part_ref[...] + turn_x(x_ref[1, 0], x_ref[1, 1], high_ref[...], low_ref[...])
    for y in range(YS):
        out_ref[y * BLOCK : (y + 1) * BLOCK, :] = turned[:, lanes_of(y)].astype(BF16)


def update_kernel(
    sum_ref, spectra_ref, weight_ref, spread_o_ref, spread_c_ref, gw_ref, sg_ref
):
    halves = [jnp.sum(sum_ref[:, half], 0) * NORM for half in range(2)]
    grad = jnp.concatenate([halves[0][:2], halves[1][:2], halves[0][2:], halves[1][2:]], 0)
    saved = jnp.concatenate([spectra_ref[:, b * 128 : (b + 1) * 128] for b in range(4)], 0)
    weight = jnp.concatenate([weight_ref[:, b * 2048 : (b + 1) * 2048] for b in range(4)], 0)
    grad_wide = sum_parts(dot(three_parts(grad), spread_o_ref[...]))
    saved_wide = sum_parts(dot(three_parts(saved), spread_c_ref[...]))

    def combine(value):
        real, imaginary = value[:4], value[4:]
        grad_real, grad_imaginary = grad_wide[:4], grad_wide[4:]
        return jnp.concatenate(
            [
                real * grad_real + imaginary * grad_imaginary,
                real * grad_imaginary - imaginary * grad_real,
            ],
            0,
        )

    outer = combine(saved_wide)
    for b in range(4):
        gw_ref[:, b * 2048 : (b + 1) * 2048] = outer[2 * b : 2 * b + 2]
    back = sum_parts(dot_last(three_parts(combine(weight)), spread_c_ref[...]))
    back = back.astype(BF16).astype(F32)
    for half in range(2):
        rows = jnp.concatenate([back[2 * half : 2 * half + 2], back[2 * half + 4 : 2 * half + 6]], 0)
        sg_ref[:, half] = jnp.broadcast_to(rows[None], (ZL * ZH, 4, QUARTER))


def turn_back(modes_ref, table_high, table_low, iy_ref, wide_ref, rhs_ref):
    for y in range(YS):
        wide_ref[:, lanes_of(y)] = modes_ref[y * BLOCK : (y + 1) * BLOCK, :]
    turned = dot(table_high, wide_ref[...]) + dot(table_low, wide_ref[...])
    for x in range(TILE_X):
        for y in range(YS):
            high, low = split(turned[x * 16 : (x + 1) * 16, lanes_of(y)])
            for at, part in enumerate((high, low, high)):
                rows = slice(at * 2 * KY + y * 16, at * 2 * KY + (y + 1) * 16)
                rhs_ref[rows, lanes_of(x)] = part
    turned = dot(iy_ref[...], rhs_ref[...])
    cells = [
        jnp.concatenate([turned[:TILE_Y, lanes_of(x)], turned[TILE_Y:, lanes_of(x)]], 1)
        for x in range(TILE_X)
    ]
    return jnp.concatenate(cells, 0)


def expand_own_kernel(
    at_ref,
    modes_ref,
    slope_ref,
    l_ref,
    high_ref,
    low_ref,
    x_ref,
    iy_ref,
    out_ref,
    wide_ref,
    rhs_ref,
):
    cells = turn_back(modes_ref, x_ref[0], x_ref[1], iy_ref, wide_ref, rhs_ref)
    high, low = split(cells)
    half = at_ref[2]
    for part in range(4):
        lanes = slice(part * 256, (part + 1) * 256)
        table = high_ref[half, :, lanes]
        out_ref[:, lanes] = (
            dot(high, table)
            + dot(low, table)
            + dot(high, low_ref[half, :, lanes])
            + dot(slope_ref[:, lanes], l_ref[...])
        )


def expand_kernel(
    at_ref,
    modes_ref,
    part_ref,
    high_ref,
    low_ref,
    x_ref,
    iy_ref,
    out_hbm,
    wide_ref,
    rhs_ref,
    out_ref,
    sems,
):
    cells = turn_back(modes_ref, x_ref[0], x_ref[1], iy_ref, wide_ref, rhs_ref)
    high, low = split(cells)
    half = 1 - at_ref[2]
    copies = []
    for part in range(4):
        lanes = slice(part * 256, (part + 1) * 256)
        table = high_ref[half, :, lanes]
        out_ref[:, lanes] = (
            dot(high, table)
            + dot(low, table)
            + dot(high, low_ref[half, :, lanes])
            + part_ref[:, lanes]
        )
        copies.append(
            pltpu.make_async_copy(out_ref.at[:, lanes], out_hbm.at[:, lanes], sems.at[part])
        )
        copies[-1].start()
    for copy in copies:
        copy.wait()


def in_vmem(count):
    return [pl.BlockSpec(memory_space=pltpu.VMEM)] * count


SMEM = pl.BlockSpec(memory_space=pltpu.SMEM)
IN_HBM = pl.BlockSpec(memory_space=pltpu.HBM)


def call(kernel, name, outs, ins, out_specs, scratch, flops=0):
    return pl.pallas_call(
        kernel,
        in_specs=ins,
        out_specs=out_specs,
        out_shape=[jax.ShapeDtypeStruct(*out) for out in outs],
        scratch_shapes=scratch,
        compiler_params=pltpu.CompilerParams(vmem_limit_bytes=20 * MIB),
        cost_estimate=pl.CostEstimate(flops=flops, bytes_accessed=4 * MIB, transcendentals=0),
        name=name,
    )


def in_hbm(value):
    return pltpu.with_memory_space_constraint(value, pltpu.HBM)


def on_device(cotangent, preact, spectra, spectral_weight, local_weight):
    table = {name: jnp.asarray(value) for name, value in tables().items()}
    place = jnp.stack(
        [lax.axis_index(("zl", "x", "c")), lax.axis_index(("zh", "y")), lax.axis_index("c")]
    ).astype(jnp.int32)
    swap = [(0, 1), (1, 0)]
    square = (ROWS, HALF)
    turn_scratch = pltpu.VMEM((6 * TILE_Y, TILE_X * QUARTER), BF16)
    cell_scratch = [pltpu.VMEM((CELLS, YS * QUARTER), BF16)] * 2

    slope, send, own_project, forward_x, inverse_x, local_map, forward_y, inverse_y = call(
        slope_kernel,
        "slope",
        [
            ((ROWS, ROW), BF16),
            (square, F32),
            ((ROW, HALF), BF16),
            ((2, 2, BLOCK, CELLS), BF16),
            ((2, CELLS, BLOCK), BF16),
            ((16 * CH, 16 * CH), BF16),
            ((2 * KY, 6 * TILE_Y), BF16),
            ((2 * TILE_Y, 6 * KY), BF16),
        ],
        [SMEM, *[IN_HBM] * 7],
        in_vmem(8),
        [
            pltpu.VMEM((ROWS, ROW), BF16),
            pltpu.VMEM((ROWS, ROW), BF16),
            pltpu.VMEM((CH, CH), BF16),
            pltpu.VMEM((2, DEPTH, HALF), BF16),
            pltpu.VMEM((2 * KX, 8 * TILE_X), BF16),
            pltpu.VMEM((ROW, HALF), BF16),
            pltpu.SemaphoreType.DMA((2, CHUNKS)),
            pltpu.SemaphoreType.DMA((5,)),
        ],
    )(
        place,
        in_hbm(cotangent.reshape(ROWS, ROW)),
        in_hbm(preact.reshape(ROWS, ROW)),
        in_hbm(local_weight),
        in_hbm(table["project"]),
        in_hbm(table["forward_x"]),
        in_hbm(table["forward_y"]),
        in_hbm(table["inverse_y"]),
    )
    depth = lax.ppermute(send, "c", swap)
    (own,) = call(
        own_kernel,
        "own_cells",
        [((BLOCK, YS * QUARTER), F32)],
        in_vmem(4),
        in_vmem(1),
        [turn_scratch, *cell_scratch],
        flops=2 * 10**9,
    )(slope, own_project, forward_x, forward_y)
    (partial,) = call(
        modes_kernel,
        "modes",
        [((2048, QUARTER), BF16)],
        in_vmem(4),
        in_vmem(1),
        [turn_scratch, *cell_scratch],
    )(depth, own, forward_x, forward_y)
    partial = lax.all_to_all(partial.reshape(16, 128, QUARTER), PLANE, 0, 0, tiled=True)
    sums = jnp.sum(partial.astype(F32), 0).reshape(32, 4, QUARTER)
    sums = lax.all_to_all(sums, LINE, 0, 0, tiled=True)
    grad_weight, back = call(
        update_kernel,
        "update",
        [((2, 8192), F32), ((ZL * ZH, CS, 4, QUARTER), F32)],
        in_vmem(5),
        in_vmem(2),
        [],
    )(
        sums.reshape(ZL * ZH, CS, 4, QUARTER),
        spectra.reshape(2, 2 * HALF),
        spectral_weight.reshape(2, 8192),
        table["spread_o"],
        table["spread_c"],
    )
    back = lax.all_to_all(back.reshape(32, 4, QUARTER).astype(BF16), LINE, 0, 0, tiled=True)
    back = jnp.broadcast_to(back.reshape(1, 128, QUARTER), (16, 128, QUARTER))
    modes = lax.all_to_all(back, PLANE, 0, 0, tiled=True).reshape(2048, QUARTER)
    other = lax.ppermute(modes, "c", swap)
    back_scratch = [pltpu.VMEM((BLOCK, YS * QUARTER), BF16), turn_scratch]
    depth_tables = (table["expand_high"], table["expand_low"])
    (part,) = call(
        expand_own_kernel,
        "expand_own",
        [((ROWS, ROW), F32)],
        [SMEM, *in_vmem(7)],
        in_vmem(1),
        back_scratch,
        flops=3 * 10**9,
    )(place, modes, slope, local_map, *depth_tables, inverse_x, inverse_y)
    (result,) = call(
        expand_kernel,
        "expand",
        [((ROWS, ROW), F32)],
        [SMEM, *in_vmem(6)],
        [IN_HBM],
        [*back_scratch, pltpu.VMEM((ROWS, ROW), F32), pltpu.SemaphoreType.DMA((4,))],
    )(place, other, part, *depth_tables, inverse_x, inverse_y)
    return result.reshape(TILE_X, TILE_Y, ROW), grad_weight.reshape(1, 2, 8192)


def solution(mesh):
    fine = Mesh(mesh.devices.reshape(ZL, XS, CS, ZH, YS), ("zl", "x", "c", "zh", "y"))
    split_spec = P(("zl", "x", "c"), ("zh", "y"), None)
    return jax.shard_map(
        on_device,
        mesh=fine,
        in_specs=(split_spec, split_spec, split_spec, split_spec, P()),
        out_specs=(split_spec, split_spec),
        check_vma=False,
    )
```

```python
import functools
import math

import jax
import jax.numpy as jnp
import ml_dtypes
import numpy as np
from jax import lax
from jax.experimental import pallas as pl
from jax.experimental.pallas import tpu as pltpu
from jax.sharding import Mesh
from jax.sharding import PartitionSpec as P

TILE_X, TILE_Y, DEPTH, CH = 16, 32, 64, 16
KX, KY, KZ = 32, 32, 16
NX, NY = 512, 512
ZL, XS, CS, ZH, YS = 4, 4, 2, 4, 4
ROW = DEPTH * CH
HALF = KZ * CH
QUARTER = 128
ROWS = TILE_X * TILE_Y
CHUNKS = 4
CHUNK_ROWS = ROWS // CHUNKS
NORM = 1.0 / math.sqrt(NX * NY * DEPTH)
F32, BF16 = jnp.float32, jnp.bfloat16
MIB = 1024 * 1024
PLANE = ("y", "x")
LINE = ("zl", "zh", "c")
FAR = 2
LINE_ORDER = [[(zl * ZH + (zh ^ FAR)) * CS + c for zl in range(ZL) for zh in range(ZH) for c in range(CS)]]
PLANE_ORDER = [[(y ^ FAR) * XS + (x ^ FAR) for y in range(YS) for x in range(XS)]]


def split_table(table):
    high = table.astype(ml_dtypes.bfloat16)
    low = (table - high.astype(np.float64)).astype(ml_dtypes.bfloat16)
    return high, low


@functools.cache
def tables():
    depth_angle = (np.outer(np.arange(DEPTH), np.arange(KZ)) % DEPTH) * (2.0 * np.pi / DEPTH)
    expand = np.stack([np.cos(depth_angle).T, -np.sin(depth_angle).T], 0) * NORM
    expand = expand.reshape(2, 2, 8, DEPTH).transpose(1, 0, 2, 3).reshape(2, KZ, DEPTH)
    expand = np.stack([np.kron(part, np.eye(CH)) for part in expand])
    expand_high, expand_low = split_table(expand)
    eye, kz8, ones = np.eye(CH), np.eye(8), np.ones((1, CH))
    spread_o = np.kron(kz8, np.kron(ones, eye)).astype(ml_dtypes.bfloat16)
    spread_c = np.kron(kz8, np.kron(eye, ones)).astype(ml_dtypes.bfloat16)
    return dict(
        expand_high=expand_high,
        expand_low=expand_low,
        spread_o=spread_o,
        spread_c=spread_c,
    )


def dot(left, right):
    return lax.dot_general(left, right, (((1,), (0,)), ((), ())), preferred_element_type=F32)


def dot_last(left, right):
    return lax.dot_general(left, right, (((1,), (1,)), ((), ())), preferred_element_type=F32)


def split(value):
    high = value.astype(BF16)
    return high, (value - high.astype(F32)).astype(BF16)


def store_split(ref, lanes, value):
    rows = value.shape[0]
    high, low = split(value)
    ref[:rows, lanes] = high
    ref[rows : 2 * rows, lanes] = low
    ref[2 * rows :, lanes] = high


def three_parts(value):
    high = value.astype(BF16)
    rest = value - high.astype(F32)
    middle = rest.astype(BF16)
    low = (rest - middle.astype(F32)).astype(BF16)
    return jnp.concatenate([high, middle, low], 0)


def sum_parts(value):
    rows = value.shape[0] // 3
    return value[:rows] + (value[rows : 2 * rows] + value[2 * rows :])


def gelu_slope(pre_value):
    normal_cdf = 0.5 * (1.0 + lax.erf(pre_value * (1.0 / math.sqrt(2.0))))
    return normal_cdf + pre_value * jnp.exp(-0.5 * pre_value * pre_value) * (
        1.0 / math.sqrt(2.0 * math.pi)
    )


def lanes_of(at):
    return slice(at * QUARTER, (at + 1) * QUARTER)


def iota(shape, axis):
    return lax.broadcasted_iota(jnp.int32, shape, axis)


def one_hot(condition):
    return condition.astype(F32).astype(BF16)


BLOCK, CELLS = 512, 256


def fill_forward(out_ref, small):
    shape = (128, 1024)
    cells = one_hot(iota(shape, 1) >> 3 == iota(shape, 0))
    shape = (128, 64)
    twice = one_hot(iota(shape, 0) >> 1 == iota(shape, 1))
    wide = dot(twice, dot(small, cells).astype(BF16))
    shape = (8, CELLS)
    local, ky = iota(shape, 0) & 1, iota(shape, 1) & 7
    masks = [(ky == 2 * zh + local).astype(F32) for zh in range(ZH)]
    for part in range(2):
        for source in range(2):
            first = (part * 2 + source) * CELLS
            for group in range(16):
                rows = wide[group * 8 : (group + 1) * 8, first : first + CELLS]
                rows = jnp.concatenate([rows * mask for mask in masks], 0).astype(BF16)
                out_ref[source, part, group * 32 : (group + 1) * 32, :] = rows


def fill_inverse(out_ref, small):
    shape = (64, BLOCK)
    row, column = iota(shape, 0), iota(shape, 1)
    modes = one_hot((column >> 5) * 4 + (column >> 1 & 3) == row)
    wide = lax.dot_general(small, modes, (((0,), (0,)), ((), ())), preferred_element_type=F32)
    shape = (8, BLOCK)
    row, column = iota(shape, 0), iota(shape, 1)
    mask = ((column >> 3 & 3) * 2 + (column & 1) == row).astype(F32)
    for part in range(2):
        for cell in range(TILE_X):
            at = part * 64 + cell * 2
            rows = [jnp.broadcast_to(wide[i : i + 1], shape) * mask for i in (at, at + 1)]
            out_ref[part, cell * 16 : (cell + 1) * 16, :] = jnp.concatenate(rows, 0).astype(BF16)


def fill_local(out_ref, local_ref):
    shape = (16 * CH, CH)
    pick = one_hot((iota(shape, 0) & (CH - 1)) == iota(shape, 1))
    full = dot_last(dot_last(pick, local_ref[...]).astype(BF16), pick)
    shape = (16 * CH, 16 * CH)
    same = iota(shape, 0) >> 4 == iota(shape, 1) >> 4
    out_ref[...] = jnp.where(same, full, 0.0).astype(BF16)


def turn(units):
    distance = jnp.abs((units + 256 & 511) - 256)
    far = distance > 128
    near = jnp.where(far, 256 - distance, distance)
    square = near.astype(F32) * (2.0 * math.pi / 512)
    square = square * square
    value = jnp.full(units.shape, 1.0 / math.factorial(12), F32)
    for power in (10, 8, 6, 4, 2, 0):
        value = value * square + (-1.0) ** (power // 2) / math.factorial(power)
    value = jnp.where(near == 128, 0.0, value)
    return jnp.where(far, -value, value)


def mode_of(ordinal):
    return jnp.where(ordinal < 16, ordinal, ordinal - 32)


def x_table(tile):
    shape = (2 * KX, 8 * TILE_X)
    row, column = iota(shape, 0), iota(shape, 1)
    mode = mode_of((row >> 2 & 3) * 8 + ((row >> 4) ^ FAR) * 2 + (row >> 1 & 1))
    cell = (tile ^ (column >> 5 & 1)) * TILE_X + (column >> 1 & 15)
    value = turn(mode * cell + 128 * ((row & 1) - (column & 1)))
    high = value.astype(BF16)
    low = (value - high.astype(F32)).astype(BF16)
    return jnp.where(column < 4 * TILE_X, high.astype(F32), low.astype(F32)).astype(BF16)


def y_table(tile, inverse):
    shape = (64, 192)
    mode, cell = iota(shape, 0), iota(shape, 1)
    column = cell
    if inverse:
        mode, cell = cell, mode
    ordinal = ((mode >> 1 & 3) ^ FAR) * 8 + ((mode >> 4 & 3) ^ FAR) * 2 + (mode & 1)
    place = tile * TILE_Y + (cell & 31)
    value = turn(mode_of(ordinal) * place + 128 * ((mode >> 3 & 1) - (cell >> 5 & 1)))
    high = value.astype(BF16)
    low = (value - high.astype(F32)).astype(BF16)
    return jnp.where(column < 128, high.astype(F32), low.astype(F32)).astype(BF16)


def fill_project(f_ref, half):
    shape = (DEPTH, HALF)
    z, column = iota(shape, 0), iota(shape, 1)
    kz = half * 8 + (column >> 4 & 7)
    factor = turn((kz * z & 63) * 8 + 128 * (column >> 7))
    factor = jnp.where(kz == 0, factor, 2.0 * factor)
    shape = (CH, HALF)
    same = iota(shape, 0) == (iota(shape, 1) & (CH - 1))
    for z in range(DEPTH):
        rows = jnp.broadcast_to(factor[z : z + 1], shape)
        f_ref[z * CH : (z + 1) * CH, :] = jnp.where(same, rows, 0.0).astype(BF16)


def place_of():
    core = lax.axis_index("c")
    x_tile = (lax.axis_index("zl") * XS + lax.axis_index("x")) * CS + core
    return x_tile, lax.axis_index("zh") * YS + lax.axis_index("y"), core


def slope_kernel(
    cot_hbm,
    pre_hbm,
    local_hbm,
    slope_ref,
    send_ref,
    own_ref,
    forward_ref,
    inverse_ref,
    l_ref,
    fy_ref,
    iy_ref,
    cot_ref,
    pre_ref,
    local_ref,
    f_ref,
    sems,
    local_sem,
):
    def copies(chunk):
        rows = pl.ds(chunk * CHUNK_ROWS, CHUNK_ROWS)
        return (
            pltpu.make_async_copy(cot_hbm.at[rows], cot_ref.at[rows], sems.at[0, chunk]),
            pltpu.make_async_copy(pre_hbm.at[rows], pre_ref.at[rows], sems.at[1, chunk]),
        )

    for chunk in range(CHUNKS):
        for copy in copies(chunk):
            copy.start()
    local_copy = pltpu.make_async_copy(local_hbm, local_ref, local_sem)
    local_copy.start()
    x_tile, y_tile, core = place_of()
    fill_project(f_ref, 1 - core)
    fill_project(own_ref, core)
    small = x_table(x_tile)
    fill_forward(forward_ref, small)
    fill_inverse(inverse_ref, small)
    fy_ref[...] = y_table(y_tile, False)
    iy_ref[...] = y_table(y_tile, True)
    local_copy.wait()
    fill_local(l_ref, local_ref)
    for chunk in range(CHUNKS):
        for copy in copies(chunk):
            copy.wait()
        rows = slice(chunk * CHUNK_ROWS, (chunk + 1) * CHUNK_ROWS)
        pre_value = pre_ref[rows, :].astype(F32)
        slope = (cot_ref[rows, :].astype(F32) * gelu_slope(pre_value)).astype(BF16)
        slope_ref[rows, :] = slope
        if (chunk + 1) * 2 % CHUNKS == 0:
            rows = slice((chunk + 1) * CHUNK_ROWS - ROWS // 2, (chunk + 1) * CHUNK_ROWS)
            send_ref[rows, :] = dot(slope_ref[rows, :], f_ref[...])


def turn_y(depth, fy_ref, rhs_ref, high_ref, low_ref):
    for x in range(TILE_X):
        block = depth[x * TILE_Y : (x + 1) * TILE_Y]
        stacked = jnp.concatenate([block[:, :QUARTER], block[:, QUARTER:]], 0)
        store_split(rhs_ref, lanes_of(x), stacked)
    turned = dot(fy_ref[...], rhs_ref[...])
    for x in range(TILE_X):
        for y in range(YS):
            high, low = split(turned[y * 16 : (y + 1) * 16, lanes_of(x)])
            high_ref[x * 16 : (x + 1) * 16, lanes_of(y)] = high
            low_ref[x * 16 : (x + 1) * 16, lanes_of(y)] = low


def turn_x(table_high, table_low, high, low):
    return dot(table_high, high) + dot(table_high, low) + dot(table_low, high)


def own_kernel(slope_ref, f_ref, x_ref, fy_ref, part_ref, rhs_ref, high_ref, low_ref):
    turn_y(dot(slope_ref[...], f_ref[...]), fy_ref, rhs_ref, high_ref, low_ref)
    part_ref[...] = turn_x(x_ref[0, 0], x_ref[0, 1], high_ref[...], low_ref[...])


def modes_kernel(depth_ref, part_ref, x_ref, fy_ref, out_ref, rhs_ref, high_ref, low_ref):
    turn_y(depth_ref[...], fy_ref, rhs_ref, high_ref, low_ref)
    turned = part_ref[...] + turn_x(x_ref[1, 0], x_ref[1, 1], high_ref[...], low_ref[...])
    for y in range(YS):
        out_ref[y * BLOCK : (y + 1) * BLOCK, :] = turned[:, lanes_of(y)].astype(BF16)


def update_kernel(
    sum_ref, spectra_ref, weight_ref, spread_o_ref, spread_c_ref, gw_ref, sg_ref
):
    halves = [jnp.sum(sum_ref[:, half], 0) * NORM for half in range(2)]
    grad = jnp.concatenate([halves[0][:2], halves[1][:2], halves[0][2:], halves[1][2:]], 0)
    saved = jnp.concatenate([spectra_ref[:, b * 128 : (b + 1) * 128] for b in range(4)], 0)
    weight = jnp.concatenate([weight_ref[:, b * 2048 : (b + 1) * 2048] for b in range(4)], 0)
    grad_wide = sum_parts(dot(three_parts(grad), spread_o_ref[...]))
    saved_wide = sum_parts(dot(three_parts(saved), spread_c_ref[...]))

    def combine(value):
        real, imaginary = value[:4], value[4:]
        grad_real, grad_imaginary = grad_wide[:4], grad_wide[4:]
        return jnp.concatenate(
            [
                real * grad_real + imaginary * grad_imaginary,
                real * grad_imaginary - imaginary * grad_real,
            ],
            0,
        )

    outer = combine(saved_wide)
    for b in range(4):
        gw_ref[:, b * 2048 : (b + 1) * 2048] = outer[2 * b : 2 * b + 2]
    back = sum_parts(dot_last(three_parts(combine(weight)), spread_c_ref[...]))
    back = back.astype(BF16).astype(F32)
    for half in range(2):
        rows = jnp.concatenate([back[2 * half : 2 * half + 2], back[2 * half + 4 : 2 * half + 6]], 0)
        sg_ref[:, half] = jnp.broadcast_to(rows[None], (ZL * ZH, 4, QUARTER))


def turn_back(modes_ref, wide_ref):
    for y in range(YS):
        wide_ref[:, lanes_of(y)] = modes_ref[y * BLOCK : (y + 1) * BLOCK, :]


def cells_of(first, count, x_ref, iy_ref, wide_ref, rhs_ref):
    rows = slice(first * 16, (first + count) * 16)
    turned = dot(x_ref[0, rows, :], wide_ref[...]) + dot(x_ref[1, rows, :], wide_ref[...])
    for x in range(count):
        for y in range(YS):
            high, low = split(turned[x * 16 : (x + 1) * 16, lanes_of(y)])
            for at, part in enumerate((high, low, high)):
                rows = slice(at * 2 * KY + y * 16, at * 2 * KY + (y + 1) * 16)
                rhs_ref[rows, lanes_of(first + x)] = part
    turned = dot(iy_ref[...], rhs_ref[:, first * QUARTER : (first + count) * QUARTER])
    cells = [
        jnp.concatenate([turned[:TILE_Y, lanes_of(x)], turned[TILE_Y:, lanes_of(x)]], 1)
        for x in range(count)
    ]
    return split(jnp.concatenate(cells, 0))


def expand_own_kernel(
    modes_ref, slope_ref, l_ref, high_ref, low_ref, x_ref, iy_ref, out_ref, wide_ref, rhs_ref
):
    turn_back(modes_ref, wide_ref)
    high, low = cells_of(0, TILE_X, x_ref, iy_ref, wide_ref, rhs_ref)
    half = lax.axis_index("c")
    for part in range(4):
        lanes = slice(part * 256, (part + 1) * 256)
        table = high_ref[half, :, lanes]
        out_ref[:, lanes] = (
            dot(high, table)
            + dot(low, table)
            + dot(high, low_ref[half, :, lanes])
            + dot(slope_ref[:, lanes], l_ref[...])
        )


def expand_kernel(
    modes_ref,
    part_ref,
    high_ref,
    low_ref,
    x_ref,
    iy_ref,
    out_hbm,
    wide_ref,
    rhs_ref,
    out_ref,
    sems,
):
    turn_back(modes_ref, wide_ref)
    half = 1 - lax.axis_index("c")
    copies = []
    for step in range(2):
        count = TILE_X // 2
        high, low = cells_of(step * count, count, x_ref, iy_ref, wide_ref, rhs_ref)
        rows = slice(step * ROWS // 2, (step + 1) * ROWS // 2)
        for part in range(4):
            lanes = slice(part * 256, (part + 1) * 256)
            table = high_ref[half, :, lanes]
            out_ref[rows, lanes] = (
                dot(high, table)
                + dot(low, table)
                + dot(high, low_ref[half, :, lanes])
                + part_ref[rows, lanes]
            )
            copy = pltpu.make_async_copy(
                out_ref.at[rows, lanes], out_hbm.at[rows, lanes], sems.at[step, part]
            )
            copy.start()
            copies.append(copy)
    for copy in copies:
        copy.wait()


def in_vmem(count):
    return [pl.BlockSpec(memory_space=pltpu.VMEM)] * count


IN_HBM = pl.BlockSpec(memory_space=pltpu.HBM)


def call(kernel, name, outs, ins, out_specs, scratch, flops=0):
    return pl.pallas_call(
        kernel,
        in_specs=ins,
        out_specs=out_specs,
        out_shape=[jax.ShapeDtypeStruct(*out) for out in outs],
        scratch_shapes=scratch,
        compiler_params=pltpu.CompilerParams(vmem_limit_bytes=20 * MIB),
        cost_estimate=pl.CostEstimate(flops=flops, bytes_accessed=4 * MIB, transcendentals=0),
        name=name,
    )


def in_hbm(value):
    return pltpu.with_memory_space_constraint(value, pltpu.HBM)


def on_device(cotangent, preact, spectra, spectral_weight, local_weight):
    table = {name: jnp.asarray(value) for name, value in tables().items()}
    swap = [(0, 1), (1, 0)]
    square = (ROWS, HALF)
    turn_scratch = pltpu.VMEM((6 * TILE_Y, TILE_X * QUARTER), BF16)
    cell_scratch = [pltpu.VMEM((CELLS, YS * QUARTER), BF16)] * 2

    slope, send, own_project, forward_x, inverse_x, local_map, forward_y, inverse_y = call(
        slope_kernel,
        "slope",
        [
            ((ROWS, ROW), BF16),
            (square, F32),
            ((ROW, HALF), BF16),
            ((2, 2, BLOCK, CELLS), BF16),
            ((2, CELLS, BLOCK), BF16),
            ((16 * CH, 16 * CH), BF16),
            ((2 * KY, 6 * TILE_Y), BF16),
            ((2 * TILE_Y, 6 * KY), BF16),
        ],
        [IN_HBM] * 3,
        in_vmem(8),
        [
            pltpu.VMEM((ROWS, ROW), BF16),
            pltpu.VMEM((ROWS, ROW), BF16),
            pltpu.VMEM((CH, CH), BF16),
            pltpu.VMEM((ROW, HALF), BF16),
            pltpu.SemaphoreType.DMA((2, CHUNKS)),
            pltpu.SemaphoreType.DMA,
        ],
    )(
        in_hbm(cotangent.reshape(ROWS, ROW)),
        in_hbm(preact.reshape(ROWS, ROW)),
        in_hbm(local_weight),
    )
    depth = lax.ppermute(send, "c", swap)
    (own,) = call(
        own_kernel,
        "own_cells",
        [((BLOCK, YS * QUARTER), F32)],
        in_vmem(4),
        in_vmem(1),
        [turn_scratch, *cell_scratch],
        flops=2 * 10**9,
    )(slope, own_project, forward_x, forward_y)
    (partial,) = call(
        modes_kernel,
        "modes",
        [((2048, QUARTER), BF16)],
        in_vmem(4),
        in_vmem(1),
        [turn_scratch, *cell_scratch],
    )(depth, own, forward_x, forward_y)
    partial = lax.all_to_all(partial.reshape(16, 128, QUARTER), PLANE, 0, 0, tiled=True, axis_index_groups=PLANE_ORDER)
    sums = jnp.sum(partial.astype(F32), 0).reshape(32, 4, QUARTER)
    sums = lax.all_to_all(sums, LINE, 0, 0, tiled=True, axis_index_groups=LINE_ORDER)
    grad_weight, back = call(
        update_kernel,
        "update",
        [((2, 8192), F32), ((ZL * ZH, CS, 4, QUARTER), F32)],
        in_vmem(5),
        in_vmem(2),
        [],
    )(
        sums.reshape(ZL * ZH, CS, 4, QUARTER),
        spectra.reshape(2, 2 * HALF),
        spectral_weight.reshape(2, 8192),
        table["spread_o"],
        table["spread_c"],
    )
    back = lax.all_to_all(
        back.reshape(32, 4, QUARTER).astype(BF16),
        LINE,
        0,
        0,
        tiled=True,
        axis_index_groups=LINE_ORDER,
    )
    back = jnp.broadcast_to(back.reshape(1, 128, QUARTER), (16, 128, QUARTER))
    modes = lax.all_to_all(back, PLANE, 0, 0, tiled=True, axis_index_groups=PLANE_ORDER).reshape(2048, QUARTER)
    other = lax.ppermute(modes, "c", swap)
    back_scratch = [pltpu.VMEM((BLOCK, YS * QUARTER), BF16), turn_scratch]
    depth_tables = (table["expand_high"], table["expand_low"])
    (part,) = call(
        expand_own_kernel,
        "expand_own",
        [((ROWS, ROW), F32)],
        in_vmem(7),
        in_vmem(1),
        back_scratch,
        flops=3 * 10**9,
    )(modes, slope, local_map, *depth_tables, inverse_x, inverse_y)
    (result,) = call(
        expand_kernel,
        "expand",
        [((ROWS, ROW), F32)],
        in_vmem(6),
        [IN_HBM],
        [*back_scratch, pltpu.VMEM((ROWS, ROW), F32), pltpu.SemaphoreType.DMA((2, 4))],
    )(other, part, *depth_tables, inverse_x, inverse_y)
    return result.reshape(TILE_X, TILE_Y, ROW), grad_weight.reshape(1, 2, 8192)


def solution(mesh):
    fine = Mesh(mesh.devices.reshape(ZL, XS, CS, ZH, YS), ("zl", "x", "c", "zh", "y"))
    split_spec = P(("zl", "x", "c"), ("zh", "y"), None)
    return jax.shard_map(
        on_device,
        mesh=fine,
        in_specs=(split_spec, split_spec, split_spec, split_spec, P()),
        out_specs=(split_spec, split_spec),
        check_vma=False,
    )
```

```python
import functools
import math

import jax
import jax.numpy as jnp
import ml_dtypes
import numpy as np
from jax import lax
from jax.experimental import pallas as pl
from jax.experimental.pallas import tpu as pltpu
from jax.sharding import Mesh
from jax.sharding import PartitionSpec as P

TILE_X, TILE_Y, DEPTH, CH = 16, 32, 64, 16
KX, KY, KZ = 32, 32, 16
NX, NY = 512, 512
ZL, XS, CS, ZH, YS = 4, 4, 2, 4, 4
ROW = DEPTH * CH
HALF = KZ * CH
QUARTER = 128
ROWS = TILE_X * TILE_Y
CHUNKS = 2
CHUNK_ROWS = ROWS // CHUNKS
NORM = 1.0 / math.sqrt(NX * NY * DEPTH)
F32, BF16 = jnp.float32, jnp.bfloat16
MIB = 1024 * 1024
PLANE = ("y", "x")
LINE = ("zl", "zh", "c")
FAR, FAR_PLANE = 2, 2
LINE_ORDER = [[(zl * ZH + (zh ^ FAR)) * CS + c for zl in range(ZL) for zh in range(ZH) for c in range(CS)]]
PLANE_ORDER = [[(y ^ FAR_PLANE) * XS + (x ^ FAR_PLANE) for y in range(YS) for x in range(XS)]]


def split_table(table):
    high = table.astype(ml_dtypes.bfloat16)
    low = (table - high.astype(np.float64)).astype(ml_dtypes.bfloat16)
    return high, low


@functools.cache
def tables():
    depth_angle = (np.outer(np.arange(DEPTH), np.arange(KZ)) % DEPTH) * (2.0 * np.pi / DEPTH)
    expand = np.stack([np.cos(depth_angle).T, -np.sin(depth_angle).T], 0) * NORM
    expand = expand.reshape(2, 2, 8, DEPTH).transpose(1, 0, 2, 3).reshape(2, KZ, DEPTH)
    expand = np.stack([np.kron(part, np.eye(CH)) for part in expand])
    expand_high, expand_low = split_table(expand)
    return dict(
        expand_high=expand_high,
        expand_low=expand_low,
    )


def dot(left, right):
    return lax.dot_general(left, right, (((1,), (0,)), ((), ())), preferred_element_type=F32)


def dot_last(left, right):
    return lax.dot_general(left, right, (((1,), (1,)), ((), ())), preferred_element_type=F32)


def split(value):
    high = value.astype(BF16)
    return high, (value - high.astype(F32)).astype(BF16)


def store_split(ref, lanes, value):
    rows = value.shape[0]
    high, low = split(value)
    ref[:rows, lanes] = high
    ref[rows : 2 * rows, lanes] = low
    ref[2 * rows :, lanes] = high


def three_parts(value):
    high = value.astype(BF16)
    rest = value - high.astype(F32)
    middle = rest.astype(BF16)
    low = (rest - middle.astype(F32)).astype(BF16)
    return jnp.concatenate([high, middle, low], 0)


def sum_parts(value):
    rows = value.shape[0] // 3
    return value[:rows] + (value[rows : 2 * rows] + value[2 * rows :])


def gelu_slope(pre_value):
    normal_cdf = 0.5 * (1.0 + lax.erf(pre_value * (1.0 / math.sqrt(2.0))))
    return normal_cdf + pre_value * jnp.exp(-0.5 * pre_value * pre_value) * (
        1.0 / math.sqrt(2.0 * math.pi)
    )


def lanes_of(at):
    return slice(at * QUARTER, (at + 1) * QUARTER)


def iota(shape, axis):
    return lax.broadcasted_iota(jnp.int32, shape, axis)


def one_hot(condition):
    return condition.astype(F32).astype(BF16)


BLOCK, CELLS = 512, 256


def fill_forward(out_ref, small):
    shape = (128, 1024)
    cells = one_hot(iota(shape, 1) >> 3 == iota(shape, 0))
    shape = (128, 64)
    twice = one_hot(iota(shape, 0) >> 1 == iota(shape, 1))
    wide = dot(twice, dot(small, cells).astype(BF16))
    shape = (8, CELLS)
    local, ky = iota(shape, 0) & 1, iota(shape, 1) & 7
    masks = [(ky == 2 * zh + local).astype(F32) for zh in range(ZH)]
    for part in range(2):
        for source in range(2):
            first = (part * 2 + source) * CELLS
            for group in range(16):
                rows = wide[group * 8 : (group + 1) * 8, first : first + CELLS]
                rows = jnp.concatenate([rows * mask for mask in masks], 0).astype(BF16)
                out_ref[source, part, group * 32 : (group + 1) * 32, :] = rows


def fill_inverse(out_ref, small):
    shape = (64, BLOCK)
    row, column = iota(shape, 0), iota(shape, 1)
    modes = one_hot((column >> 5) * 4 + (column >> 1 & 3) == row)
    wide = lax.dot_general(small, modes, (((0,), (0,)), ((), ())), preferred_element_type=F32)
    shape = (8, BLOCK)
    row, column = iota(shape, 0), iota(shape, 1)
    mask = ((column >> 3 & 3) * 2 + (column & 1) == row).astype(F32)
    for part in range(2):
        for cell in range(TILE_X):
            at = part * 64 + cell * 2
            rows = [jnp.broadcast_to(wide[i : i + 1], shape) * mask for i in (at, at + 1)]
            out_ref[part, cell * 16 : (cell + 1) * 16, :] = jnp.concatenate(rows, 0).astype(BF16)


def fill_local(out_ref, local_ref):
    shape = (16 * CH, CH)
    pick = one_hot((iota(shape, 0) & (CH - 1)) == iota(shape, 1))
    full = dot_last(dot_last(pick, local_ref[...]).astype(BF16), pick)
    shape = (16 * CH, 16 * CH)
    same = iota(shape, 0) >> 4 == iota(shape, 1) >> 4
    out_ref[...] = jnp.where(same, full, 0.0).astype(BF16)


def turn(units):
    distance = jnp.abs((units + 256 & 511) - 256)
    far = distance > 128
    near = jnp.where(far, 256 - distance, distance)
    square = near.astype(F32) * (2.0 * math.pi / 512)
    square = square * square
    value = jnp.full(units.shape, 1.0 / math.factorial(12), F32)
    for power in (10, 8, 6, 4, 2, 0):
        value = value * square + (-1.0) ** (power // 2) / math.factorial(power)
    value = jnp.where(near == 128, 0.0, value)
    return jnp.where(far, -value, value)


def mode_of(ordinal):
    return jnp.where(ordinal < 16, ordinal, ordinal - 32)


def x_table(tile):
    shape = (2 * KX, 8 * TILE_X)
    row, column = iota(shape, 0), iota(shape, 1)
    mode = mode_of((row >> 2 & 3) * 8 + ((row >> 4) ^ FAR_PLANE) * 2 + (row >> 1 & 1))
    cell = (tile ^ (column >> 5 & 1)) * TILE_X + (column >> 1 & 15)
    value = turn(mode * cell + 128 * ((row & 1) - (column & 1)))
    high = value.astype(BF16)
    low = (value - high.astype(F32)).astype(BF16)
    return jnp.where(column < 4 * TILE_X, high.astype(F32), low.astype(F32)).astype(BF16)


def y_table(tile, inverse):
    shape = (64, 192)
    mode, cell = iota(shape, 0), iota(shape, 1)
    column = cell
    if inverse:
        mode, cell = cell, mode
    ordinal = ((mode >> 1 & 3) ^ FAR) * 8 + ((mode >> 4 & 3) ^ FAR_PLANE) * 2 + (mode & 1)
    place = tile * TILE_Y + (cell & 31)
    value = turn(mode_of(ordinal) * place + 128 * ((mode >> 3 & 1) - (cell >> 5 & 1)))
    high = value.astype(BF16)
    low = (value - high.astype(F32)).astype(BF16)
    return jnp.where(column < 128, high.astype(F32), low.astype(F32)).astype(BF16)


def fill_project(f_ref, half):
    shape = (DEPTH, HALF)
    z, column = iota(shape, 0), iota(shape, 1)
    kz = half * 8 + (column >> 4 & 7)
    factor = turn((kz * z & 63) * 8 + 128 * (column >> 7))
    factor = jnp.where(kz == 0, factor, 2.0 * factor)
    shape = (CH, HALF)
    same = iota(shape, 0) == (iota(shape, 1) & (CH - 1))
    for z in range(DEPTH):
        rows = jnp.broadcast_to(factor[z : z + 1], shape)
        f_ref[z * CH : (z + 1) * CH, :] = jnp.where(same, rows, 0.0).astype(BF16)


def place_of():
    core = lax.axis_index("c")
    x_tile = (lax.axis_index("zl") * XS + lax.axis_index("x")) * CS + core
    return x_tile, lax.axis_index("zh") * YS + lax.axis_index("y"), core


def slope_kernel(cot_hbm, pre_hbm, slope_ref, send_ref, cot_ref, pre_ref, f_ref, sems):
    def copies(chunk):
        rows = pl.ds(chunk * CHUNK_ROWS, CHUNK_ROWS)
        return (
            pltpu.make_async_copy(cot_hbm.at[rows], cot_ref.at[rows], sems.at[0, chunk]),
            pltpu.make_async_copy(pre_hbm.at[rows], pre_ref.at[rows], sems.at[1, chunk]),
        )

    for chunk in range(CHUNKS):
        for copy in copies(chunk):
            copy.start()
    fill_project(f_ref, 1 - lax.axis_index("c"))
    for chunk in range(CHUNKS):
        for copy in copies(chunk):
            copy.wait()
        rows = slice(chunk * CHUNK_ROWS, (chunk + 1) * CHUNK_ROWS)
        pre_value = pre_ref[rows, :].astype(F32)
        slope = (cot_ref[rows, :].astype(F32) * gelu_slope(pre_value)).astype(BF16)
        slope_ref[rows, :] = slope
        send_ref[rows, :] = dot(slope_ref[rows, :], f_ref[...])


def turn_y(depth, fy_ref, rhs_ref, high_ref, low_ref):
    for x in range(TILE_X):
        block = depth[x * TILE_Y : (x + 1) * TILE_Y]
        stacked = jnp.concatenate([block[:, :QUARTER], block[:, QUARTER:]], 0)
        store_split(rhs_ref, lanes_of(x), stacked)
    turned = dot(fy_ref[...], rhs_ref[...])
    for x in range(TILE_X):
        for y in range(YS):
            high, low = split(turned[y * 16 : (y + 1) * 16, lanes_of(x)])
            high_ref[x * 16 : (x + 1) * 16, lanes_of(y)] = high
            low_ref[x * 16 : (x + 1) * 16, lanes_of(y)] = low


def turn_x(table_high, table_low, high, low):
    return dot(table_high, high) + dot(table_high, low) + dot(table_low, high)


def own_kernel(
    slope_ref,
    local_ref,
    part_ref,
    forward_ref,
    inverse_ref,
    l_ref,
    fy_ref,
    iy_ref,
    f_ref,
    depth_ref,
    rhs_ref,
    high_ref,
    low_ref,
):
    x_tile, y_tile, core = place_of()
    fill_project(f_ref, core)
    for chunk in range(4):
        rows = slice(chunk * ROWS // 4, (chunk + 1) * ROWS // 4)
        depth_ref[rows, :] = dot(slope_ref[rows, :], f_ref[...])
    fy_ref[...] = y_table(y_tile, False)
    iy_ref[...] = y_table(y_tile, True)
    small = x_table(x_tile)
    fill_forward(forward_ref, small)
    fill_inverse(inverse_ref, small)
    fill_local(l_ref, local_ref)
    turn_y(depth_ref[...], fy_ref, rhs_ref, high_ref, low_ref)
    for part in range(2):
        lanes = slice(part * 256, (part + 1) * 256)
        part_ref[:, lanes] = turn_x(
            forward_ref[0, 0], forward_ref[0, 1], high_ref[:, lanes], low_ref[:, lanes]
        )


def modes_kernel(depth_ref, part_ref, x_ref, fy_ref, out_ref, rhs_ref, high_ref, low_ref):
    turn_y(depth_ref[...], fy_ref, rhs_ref, high_ref, low_ref)
    turned = part_ref[...] + turn_x(x_ref[1, 0], x_ref[1, 1], high_ref[...], low_ref[...])
    for y in range(YS):
        out_ref[y * BLOCK : (y + 1) * BLOCK, :] = turned[:, lanes_of(y)].astype(BF16)


def update_kernel(sum_ref, spectra_ref, weight_ref, gw_ref, sg_ref):
    halves = [jnp.sum(sum_ref[:, half], 0) * NORM for half in range(2)]
    grad = jnp.concatenate([halves[0][:2], halves[1][:2], halves[0][2:], halves[1][2:]], 0)
    saved = jnp.concatenate([spectra_ref[:, b * 128 : (b + 1) * 128] for b in range(4)], 0)
    shape = (64, QUARTER)
    own_kz = iota(shape, 0) >> 3 == iota(shape, 1) >> 4
    shape = (QUARTER, CH * CH)
    row, column = iota(shape, 0) & (CH - 1), iota(shape, 1)
    spread_c = one_hot(row == column >> 4)
    spread_o = one_hot(row == (column & (CH - 1)))

    def spread(value, table):
        rows = jnp.where(own_kz, jnp.concatenate([value] * 8, 0), 0.0)
        return sum_parts(dot(three_parts(rows), table))

    grad_wide, saved_wide = spread(grad, spread_o), spread(saved, spread_c)
    weight = jnp.concatenate(
        [
            weight_ref[:, b * 2048 + kz * 256 : b * 2048 + (kz + 1) * 256]
            for kz in range(8)
            for b in range(4)
        ],
        0,
    )
    real_rows = (iota((64, CH * CH), 0) & 4) == 0

    def combine(value):
        product = value * grad_wide
        crossed = swap_parts(value) * grad_wide
        return jnp.where(
            real_rows, product + swap_parts(product), crossed - swap_parts(crossed)
        )

    def swap_parts(value):
        return jnp.where(real_rows, pltpu.roll(value, 60, 0), pltpu.roll(value, 4, 0))

    outer = combine(saved_wide)
    for kz in range(8):
        for b in range(4):
            lanes = slice(b * 2048 + kz * 256, b * 2048 + (kz + 1) * 256)
            gw_ref[:, lanes] = outer[kz * 8 + b * 2 : kz * 8 + b * 2 + 2]
    back = sum_parts(dot_last(three_parts(combine(weight)), spread_c))
    back = jnp.where(own_kz, back, 0.0)
    back = functools.reduce(jnp.add, [back[kz * 8 : (kz + 1) * 8] for kz in range(8)])
    back = back.astype(BF16).astype(F32)
    for half in range(2):
        rows = jnp.concatenate([back[2 * half : 2 * half + 2], back[2 * half + 4 : 2 * half + 6]], 0)
        sg_ref[:, half] = jnp.broadcast_to(rows[None], (ZL * ZH, 4, QUARTER))


def turn_back(modes_ref, wide_ref):
    for y in range(YS):
        wide_ref[:, lanes_of(y)] = modes_ref[y * BLOCK : (y + 1) * BLOCK, :]


def cells_of(first, count, x_ref, iy_ref, wide_ref, rhs_ref):
    rows = slice(first * 16, (first + count) * 16)
    turned = dot(x_ref[0, rows, :], wide_ref[...]) + dot(x_ref[1, rows, :], wide_ref[...])
    for x in range(count):
        for y in range(YS):
            high, low = split(turned[x * 16 : (x + 1) * 16, lanes_of(y)])
            for at, part in enumerate((high, low, high)):
                rows = slice(at * 2 * KY + y * 16, at * 2 * KY + (y + 1) * 16)
                rhs_ref[rows, lanes_of(first + x)] = part
    turned = dot(iy_ref[...], rhs_ref[:, first * QUARTER : (first + count) * QUARTER])
    cells = [
        jnp.concatenate([turned[:TILE_Y, lanes_of(x)], turned[TILE_Y:, lanes_of(x)]], 1)
        for x in range(count)
    ]
    return split(jnp.concatenate(cells, 0))


def expand_own_kernel(
    modes_ref, slope_ref, l_ref, high_ref, low_ref, x_ref, iy_ref, out_ref, wide_ref, rhs_ref
):
    turn_back(modes_ref, wide_ref)
    high, low = cells_of(0, TILE_X, x_ref, iy_ref, wide_ref, rhs_ref)
    half = lax.axis_index("c")
    for part in range(4):
        lanes = slice(part * 256, (part + 1) * 256)
        table = high_ref[half, :, lanes]
        out_ref[:, lanes] = (
            dot(high, table)
            + dot(low, table)
            + dot(high, low_ref[half, :, lanes])
            + dot(slope_ref[:, lanes], l_ref[...])
        )


def expand_kernel(
    modes_ref,
    part_ref,
    high_ref,
    low_ref,
    x_ref,
    iy_ref,
    gw_ref,
    out_hbm,
    gw_hbm,
    wide_ref,
    rhs_ref,
    out_ref,
    sems,
    gw_sem,
):
    gw_copy = pltpu.make_async_copy(gw_ref, gw_hbm, gw_sem)
    gw_copy.start()
    turn_back(modes_ref, wide_ref)
    half = 1 - lax.axis_index("c")
    copies = [gw_copy]
    high, low = cells_of(0, TILE_X, x_ref, iy_ref, wide_ref, rhs_ref)
    for part in range(4):
        lanes = slice(part * 256, (part + 1) * 256)
        table = high_ref[half, :, lanes]
        out_ref[:, lanes] = (
            dot(high, table)
            + dot(low, table)
            + dot(high, low_ref[half, :, lanes])
            + part_ref[:, lanes]
        )
        copy = pltpu.make_async_copy(out_ref.at[:, lanes], out_hbm.at[:, lanes], sems.at[part])
        copy.start()
        copies.append(copy)
    for copy in copies:
        copy.wait()


def in_vmem(count):
    return [pl.BlockSpec(memory_space=pltpu.VMEM)] * count


IN_HBM = pl.BlockSpec(memory_space=pltpu.HBM)


def call(kernel, name, outs, ins, out_specs, scratch, flops=0):
    return pl.pallas_call(
        kernel,
        in_specs=ins,
        out_specs=out_specs,
        out_shape=[jax.ShapeDtypeStruct(*out) for out in outs],
        scratch_shapes=scratch,
        compiler_params=pltpu.CompilerParams(vmem_limit_bytes=20 * MIB),
        cost_estimate=pl.CostEstimate(flops=flops, bytes_accessed=4 * MIB, transcendentals=0),
        name=name,
    )


def in_hbm(value):
    return pltpu.with_memory_space_constraint(value, pltpu.HBM)


def on_device(cotangent, preact, spectra, spectral_weight, local_weight):
    table = {name: jnp.asarray(value) for name, value in tables().items()}
    swap = [(0, 1), (1, 0)]
    square = (ROWS, HALF)
    turn_scratch = pltpu.VMEM((6 * TILE_Y, TILE_X * QUARTER), BF16)
    cell_scratch = [pltpu.VMEM((CELLS, YS * QUARTER), BF16)] * 2

    slope, send = call(
        slope_kernel,
        "slope",
        [((ROWS, ROW), BF16), (square, F32)],
        [IN_HBM] * 2,
        in_vmem(2),
        [
            pltpu.VMEM((ROWS, ROW), BF16),
            pltpu.VMEM((ROWS, ROW), BF16),
            pltpu.VMEM((ROW, HALF), BF16),
            pltpu.SemaphoreType.DMA((2, CHUNKS)),
        ],
    )(in_hbm(cotangent.reshape(ROWS, ROW)), in_hbm(preact.reshape(ROWS, ROW)))
    depth = lax.ppermute(send, "c", swap)
    own, forward_x, inverse_x, local_map, forward_y, inverse_y = call(
        own_kernel,
        "own_cells",
        [
            ((BLOCK, YS * QUARTER), F32),
            ((2, 2, BLOCK, CELLS), BF16),
            ((2, CELLS, BLOCK), BF16),
            ((16 * CH, 16 * CH), BF16),
            ((2 * KY, 6 * TILE_Y), BF16),
            ((2 * TILE_Y, 6 * KY), BF16),
        ],
        in_vmem(2),
        in_vmem(6),
        [pltpu.VMEM((ROW, HALF), BF16), pltpu.VMEM(square, F32), turn_scratch, *cell_scratch],
        flops=2 * 10**9,
    )(slope, local_weight)
    (partial,) = call(
        modes_kernel,
        "modes",
        [((2048, QUARTER), BF16)],
        in_vmem(4),
        in_vmem(1),
        [turn_scratch, *cell_scratch],
    )(depth, own, forward_x, forward_y)
    partial = lax.all_to_all(partial.reshape(16, 128, QUARTER), PLANE, 0, 0, tiled=True, axis_index_groups=PLANE_ORDER)
    sums = jnp.sum(partial.astype(F32), 0).reshape(32, 4, QUARTER)
    sums = lax.all_to_all(sums, LINE, 0, 0, tiled=True, axis_index_groups=LINE_ORDER)
    grad_weight, back = call(
        update_kernel,
        "update",
        [((2, 8192), F32), ((ZL * ZH, CS, 4, QUARTER), F32)],
        in_vmem(3),
        in_vmem(2),
        [],
    )(
        sums.reshape(ZL * ZH, CS, 4, QUARTER),
        spectra.reshape(2, 2 * HALF),
        spectral_weight.reshape(2, 8192),
    )
    back = lax.all_to_all(
        back.reshape(32, 4, QUARTER).astype(BF16),
        LINE,
        0,
        0,
        tiled=True,
        axis_index_groups=LINE_ORDER,
    )
    back = jnp.broadcast_to(back.reshape(1, 128, QUARTER), (16, 128, QUARTER))
    modes = lax.all_to_all(back, PLANE, 0, 0, tiled=True, axis_index_groups=PLANE_ORDER).reshape(2048, QUARTER)
    other = lax.ppermute(modes, "c", swap)
    back_scratch = [pltpu.VMEM((BLOCK, YS * QUARTER), BF16), turn_scratch]
    depth_tables = (table["expand_high"], table["expand_low"])
    (part,) = call(
        expand_own_kernel,
        "expand_own",
        [((ROWS, ROW), F32)],
        in_vmem(7),
        in_vmem(1),
        back_scratch,
        flops=3 * 10**9,
    )(modes, slope, local_map, *depth_tables, inverse_x, inverse_y)
    result, grad_weight = call(
        expand_kernel,
        "expand",
        [((ROWS, ROW), F32), ((2, 8192), F32)],
        in_vmem(7),
        [IN_HBM, IN_HBM],
        [
            *back_scratch,
            pltpu.VMEM((ROWS, ROW), F32),
            pltpu.SemaphoreType.DMA((4,)),
            pltpu.SemaphoreType.DMA,
        ],
    )(other, part, *depth_tables, inverse_x, inverse_y, grad_weight)
    return result.reshape(TILE_X, TILE_Y, ROW), grad_weight.reshape(1, 2, 8192)


def solution(mesh):
    fine = Mesh(mesh.devices.reshape(ZL, XS, CS, ZH, YS), ("zl", "x", "c", "zh", "y"))
    split_spec = P(("zl", "x", "c"), ("zh", "y"), None)
    return jax.shard_map(
        on_device,
        mesh=fine,
        in_specs=(split_spec, split_spec, split_spec, split_spec, P()),
        out_specs=(split_spec, split_spec),
        check_vma=False,
    )
```

```python
import functools
import math

import jax
import jax.numpy as jnp
import ml_dtypes
import numpy as np
from jax import lax
from jax.experimental import pallas as pl
from jax.experimental.pallas import tpu as pltpu
from jax.sharding import Mesh
from jax.sharding import PartitionSpec as P

TILE_X, TILE_Y, DEPTH, CH = 16, 32, 64, 16
KX, KY, KZ = 32, 32, 16
NX, NY = 512, 512
ZL, XS, CS, ZH, YS = 4, 4, 2, 4, 4
ROW = DEPTH * CH
HALF = KZ * CH
QUARTER = 128
ROWS = TILE_X * TILE_Y
CHUNKS = 2
CHUNK_ROWS = ROWS // CHUNKS
NORM = 1.0 / math.sqrt(NX * NY * DEPTH)
F32, BF16 = jnp.float32, jnp.bfloat16
MIB = 1024 * 1024
PLANE = ("y", "x")
LINE = ("zl", "zh", "c")
FAR, FAR_PLANE = 2, 2
LINE_ORDER = [[(zl * ZH + (zh ^ FAR)) * CS + c for zl in range(ZL) for zh in range(ZH) for c in range(CS)]]
PLANE_ORDER = [[(y ^ FAR_PLANE) * XS + (x ^ FAR_PLANE) for y in range(YS) for x in range(XS)]]


def split_table(table):
    high = table.astype(ml_dtypes.bfloat16)
    low = (table - high.astype(np.float64)).astype(ml_dtypes.bfloat16)
    return high, low


@functools.cache
def tables():
    depth_angle = (np.outer(np.arange(DEPTH), np.arange(KZ)) % DEPTH) * (2.0 * np.pi / DEPTH)
    expand = np.stack([np.cos(depth_angle).T, -np.sin(depth_angle).T], 0) * NORM
    expand = expand.reshape(2, 2, 8, DEPTH).transpose(1, 0, 2, 3).reshape(2, KZ, DEPTH)
    expand = np.stack([np.kron(part, np.eye(CH)) for part in expand])
    expand = np.stack(split_table(expand), 1)
    return dict(
        expand=expand,
    )


def dot(left, right):
    return lax.dot_general(left, right, (((1,), (0,)), ((), ())), preferred_element_type=F32)


def dot_last(left, right):
    return lax.dot_general(left, right, (((1,), (1,)), ((), ())), preferred_element_type=F32)


def split(value):
    high = value.astype(BF16)
    return high, (value - high.astype(F32)).astype(BF16)


def store_split(ref, lanes, value):
    rows = value.shape[0]
    high, low = split(value)
    ref[:rows, lanes] = high
    ref[rows : 2 * rows, lanes] = low
    ref[2 * rows :, lanes] = high


def three_parts(value):
    high = value.astype(BF16)
    rest = value - high.astype(F32)
    middle = rest.astype(BF16)
    low = (rest - middle.astype(F32)).astype(BF16)
    return jnp.concatenate([high, middle, low], 0)


def sum_parts(value):
    rows = value.shape[0] // 3
    return value[:rows] + (value[rows : 2 * rows] + value[2 * rows :])


def gelu_slope(pre_value):
    normal_cdf = 0.5 * (1.0 + lax.erf(pre_value * (1.0 / math.sqrt(2.0))))
    return normal_cdf + pre_value * jnp.exp(-0.5 * pre_value * pre_value) * (
        1.0 / math.sqrt(2.0 * math.pi)
    )


def lanes_of(at):
    return slice(at * QUARTER, (at + 1) * QUARTER)


def iota(shape, axis):
    return lax.broadcasted_iota(jnp.int32, shape, axis)


def one_hot(condition):
    return condition.astype(F32).astype(BF16)


BLOCK, CELLS = 512, 256


def fill_forward(out_ref, small):
    shape = (128, 1024)
    cells = one_hot(iota(shape, 1) >> 3 == iota(shape, 0))
    shape = (128, 64)
    twice = one_hot(iota(shape, 0) >> 1 == iota(shape, 1))
    wide = dot(twice, dot(small, cells).astype(BF16))
    shape = (8, CELLS)
    local, ky = iota(shape, 0) & 1, iota(shape, 1) & 7
    masks = [(ky == 2 * zh + local).astype(F32) for zh in range(ZH)]
    for part in range(2):
        for source in range(2):
            first = (part * 2 + source) * CELLS
            for group in range(16):
                rows = wide[group * 8 : (group + 1) * 8, first : first + CELLS]
                rows = jnp.concatenate([rows * mask for mask in masks], 0).astype(BF16)
                out_ref[source, part, group * 32 : (group + 1) * 32, :] = rows


def fill_inverse(out_ref, small):
    shape = (64, BLOCK)
    row, column = iota(shape, 0), iota(shape, 1)
    modes = one_hot((column >> 5) * 4 + (column >> 1 & 3) == row)
    wide = lax.dot_general(small, modes, (((0,), (0,)), ((), ())), preferred_element_type=F32)
    shape = (8, BLOCK)
    row, column = iota(shape, 0), iota(shape, 1)
    mask = ((column >> 3 & 3) * 2 + (column & 1) == row).astype(F32)
    for part in range(2):
        for cell in range(TILE_X):
            at = part * 64 + cell * 2
            rows = [jnp.broadcast_to(wide[i : i + 1], shape) * mask for i in (at, at + 1)]
            out_ref[part, cell * 16 : (cell + 1) * 16, :] = jnp.concatenate(rows, 0).astype(BF16)


def fill_local(out_ref, local_ref):
    shape = (16 * CH, CH)
    pick = one_hot((iota(shape, 0) & (CH - 1)) == iota(shape, 1))
    full = dot_last(dot_last(pick, local_ref[...]).astype(BF16), pick)
    shape = (16 * CH, 16 * CH)
    same = iota(shape, 0) >> 4 == iota(shape, 1) >> 4
    out_ref[...] = jnp.where(same, full, 0.0).astype(BF16)


def turn(units):
    distance = jnp.abs((units + 256 & 511) - 256)
    far = distance > 128
    near = jnp.where(far, 256 - distance, distance)
    square = near.astype(F32) * (2.0 * math.pi / 512)
    square = square * square
    value = jnp.full(units.shape, 1.0 / math.factorial(12), F32)
    for power in (10, 8, 6, 4, 2, 0):
        value = value * square + (-1.0) ** (power // 2) / math.factorial(power)
    value = jnp.where(near == 128, 0.0, value)
    return jnp.where(far, -value, value)


def mode_of(ordinal):
    return jnp.where(ordinal < 16, ordinal, ordinal - 32)


def x_table(tile):
    shape = (2 * KX, 8 * TILE_X)
    row, column = iota(shape, 0), iota(shape, 1)
    mode = mode_of((row >> 2 & 3) * 8 + ((row >> 4) ^ FAR_PLANE) * 2 + (row >> 1 & 1))
    cell = (tile ^ (column >> 5 & 1)) * TILE_X + (column >> 1 & 15)
    value = turn(mode * cell + 128 * ((row & 1) - (column & 1)))
    high = value.astype(BF16)
    low = (value - high.astype(F32)).astype(BF16)
    return jnp.where(column < 4 * TILE_X, high.astype(F32), low.astype(F32)).astype(BF16)


def y_table(tile, inverse):
    shape = (64, 192)
    mode, cell = iota(shape, 0), iota(shape, 1)
    column = cell
    if inverse:
        mode, cell = cell, mode
    ordinal = ((mode >> 1 & 3) ^ FAR) * 8 + ((mode >> 4 & 3) ^ FAR_PLANE) * 2 + (mode & 1)
    place = tile * TILE_Y + (cell & 31)
    value = turn(mode_of(ordinal) * place + 128 * ((mode >> 3 & 1) - (cell >> 5 & 1)))
    high = value.astype(BF16)
    low = (value - high.astype(F32)).astype(BF16)
    return jnp.where(column < 128, high.astype(F32), low.astype(F32)).astype(BF16)


def fill_project(f_ref, half):
    shape = (DEPTH, HALF)
    z, column = iota(shape, 0), iota(shape, 1)
    kz = half * 8 + (column >> 4 & 7)
    factor = turn((kz * z & 63) * 8 + 128 * (column >> 7))
    factor = jnp.where(kz == 0, factor, 2.0 * factor)
    shape = (CH, HALF)
    same = iota(shape, 0) == (iota(shape, 1) & (CH - 1))
    for z in range(DEPTH):
        rows = jnp.broadcast_to(factor[z : z + 1], shape)
        f_ref[z * CH : (z + 1) * CH, :] = jnp.where(same, rows, 0.0).astype(BF16)


def place_of():
    core = lax.axis_index("c")
    x_tile = (lax.axis_index("zl") * XS + lax.axis_index("x")) * CS + core
    return x_tile, lax.axis_index("zh") * YS + lax.axis_index("y"), core


def slope_kernel(cot_hbm, pre_hbm, slope_ref, send_ref, cot_ref, pre_ref, f_ref, sems):
    def copies(chunk):
        rows = pl.ds(chunk * CHUNK_ROWS, CHUNK_ROWS)
        return (
            pltpu.make_async_copy(cot_hbm.at[rows], cot_ref.at[rows], sems.at[0, chunk]),
            pltpu.make_async_copy(pre_hbm.at[rows], pre_ref.at[rows], sems.at[1, chunk]),
        )

    for chunk in range(CHUNKS):
        for copy in copies(chunk):
            copy.start()
    fill_project(f_ref, 1 - lax.axis_index("c"))
    for chunk in range(CHUNKS):
        for copy in copies(chunk):
            copy.wait()
        rows = slice(chunk * CHUNK_ROWS, (chunk + 1) * CHUNK_ROWS)
        pre_value = pre_ref[rows, :].astype(F32)
        slope = (cot_ref[rows, :].astype(F32) * gelu_slope(pre_value)).astype(BF16)
        slope_ref[rows, :] = slope
        send_ref[rows, :] = dot(slope_ref[rows, :], f_ref[...])


def turn_y(depth, fy_ref, rhs_ref, high_ref, low_ref):
    for x in range(TILE_X):
        block = depth[x * TILE_Y : (x + 1) * TILE_Y]
        stacked = jnp.concatenate([block[:, :QUARTER], block[:, QUARTER:]], 0)
        store_split(rhs_ref, lanes_of(x), stacked)
    turned = dot(fy_ref[...], rhs_ref[...])
    for x in range(TILE_X):
        for y in range(YS):
            high, low = split(turned[y * 16 : (y + 1) * 16, lanes_of(x)])
            high_ref[x * 16 : (x + 1) * 16, lanes_of(y)] = high
            low_ref[x * 16 : (x + 1) * 16, lanes_of(y)] = low


def turn_x(table_high, table_low, high, low):
    return dot(table_high, high) + dot(table_high, low) + dot(table_low, high)


def own_kernel(
    slope_ref,
    local_ref,
    part_ref,
    forward_ref,
    inverse_ref,
    l_ref,
    fy_ref,
    iy_ref,
    f_ref,
    depth_ref,
    rhs_ref,
    high_ref,
    low_ref,
):
    x_tile, y_tile, core = place_of()
    fill_project(f_ref, core)
    for chunk in range(4):
        rows = slice(chunk * ROWS // 4, (chunk + 1) * ROWS // 4)
        depth_ref[rows, :] = dot(slope_ref[rows, :], f_ref[...])
    fy_ref[...] = y_table(y_tile, False)
    iy_ref[...] = y_table(y_tile, True)
    small = x_table(x_tile)
    fill_forward(forward_ref, small)
    fill_inverse(inverse_ref, small)
    fill_local(l_ref, local_ref)
    turn_y(depth_ref[...], fy_ref, rhs_ref, high_ref, low_ref)
    for part in range(2):
        lanes = slice(part * 256, (part + 1) * 256)
        part_ref[:, lanes] = turn_x(
            forward_ref[0, 0], forward_ref[0, 1], high_ref[:, lanes], low_ref[:, lanes]
        )


def modes_kernel(depth_ref, part_ref, x_ref, fy_ref, out_ref, rhs_ref, high_ref, low_ref):
    turn_y(depth_ref[...], fy_ref, rhs_ref, high_ref, low_ref)
    turned = part_ref[...] + turn_x(x_ref[1, 0], x_ref[1, 1], high_ref[...], low_ref[...])
    for y in range(YS):
        out_ref[y * BLOCK : (y + 1) * BLOCK, :] = turned[:, lanes_of(y)].astype(BF16)


def sum_kernel(part_ref, out_ref):
    out_ref[...] = jnp.sum(part_ref[...].astype(F32), 0).astype(BF16)


def update_kernel(sum_ref, spectra_ref, weight_ref, gw_ref, sg_ref):
    halves = [jnp.sum(sum_ref[:, half].astype(F32), 0) * NORM for half in range(2)]
    grad = jnp.concatenate([halves[0][:2], halves[1][:2], halves[0][2:], halves[1][2:]], 0)
    saved = jnp.concatenate([spectra_ref[:, b * 128 : (b + 1) * 128] for b in range(4)], 0)
    shape = (64, QUARTER)
    own_kz = iota(shape, 0) >> 3 == iota(shape, 1) >> 4
    shape = (QUARTER, CH * CH)
    row, column = iota(shape, 0) & (CH - 1), iota(shape, 1)
    spread_c = one_hot(row == column >> 4)
    spread_o = one_hot(row == (column & (CH - 1)))

    def spread(value, table):
        rows = jnp.where(own_kz, jnp.concatenate([value] * 8, 0), 0.0)
        return sum_parts(dot(three_parts(rows), table))

    grad_wide, saved_wide = spread(grad, spread_o), spread(saved, spread_c)
    weight = jnp.concatenate(
        [
            weight_ref[:, b * 2048 + kz * 256 : b * 2048 + (kz + 1) * 256]
            for kz in range(8)
            for b in range(4)
        ],
        0,
    )
    real_rows = (iota((64, CH * CH), 0) & 4) == 0

    def combine(value):
        product = value * grad_wide
        crossed = swap_parts(value) * grad_wide
        return jnp.where(
            real_rows, product + swap_parts(product), crossed - swap_parts(crossed)
        )

    def swap_parts(value):
        return jnp.where(real_rows, pltpu.roll(value, 60, 0), pltpu.roll(value, 4, 0))

    outer = combine(saved_wide)
    for kz in range(8):
        for b in range(4):
            lanes = slice(b * 2048 + kz * 256, b * 2048 + (kz + 1) * 256)
            gw_ref[:, lanes] = outer[kz * 8 + b * 2 : kz * 8 + b * 2 + 2]
    back = sum_parts(dot_last(three_parts(combine(weight)), spread_c))
    back = jnp.where(own_kz, back, 0.0)
    back = functools.reduce(jnp.add, [back[kz * 8 : (kz + 1) * 8] for kz in range(8)])
    back = back.astype(BF16).astype(F32)
    for half in range(2):
        rows = jnp.concatenate([back[2 * half : 2 * half + 2], back[2 * half + 4 : 2 * half + 6]], 0)
        sg_ref[:, half] = jnp.broadcast_to(rows[None], (ZL * ZH, 4, QUARTER))


def turn_back(modes_ref, wide_ref):
    for y in range(YS):
        wide_ref[:, lanes_of(y)] = modes_ref[y * BLOCK : (y + 1) * BLOCK, :]


def cells_of(first, count, x_ref, iy_ref, wide_ref, rhs_ref):
    rows = slice(first * 16, (first + count) * 16)
    turned = dot(x_ref[0, rows, :], wide_ref[...]) + dot(x_ref[1, rows, :], wide_ref[...])
    for x in range(count):
        for y in range(YS):
            high, low = split(turned[x * 16 : (x + 1) * 16, lanes_of(y)])
            for at, part in enumerate((high, low, high)):
                rows = slice(at * 2 * KY + y * 16, at * 2 * KY + (y + 1) * 16)
                rhs_ref[rows, lanes_of(first + x)] = part
    turned = dot(iy_ref[...], rhs_ref[:, first * QUARTER : (first + count) * QUARTER])
    cells = [
        jnp.concatenate([turned[:TILE_Y, lanes_of(x)], turned[TILE_Y:, lanes_of(x)]], 1)
        for x in range(count)
    ]
    return split(jnp.concatenate(cells, 0))


def expand_own_kernel(
    modes_ref, slope_ref, l_ref, depth_ref, x_ref, iy_ref, out_ref, wide_ref, rhs_ref
):
    turn_back(modes_ref, wide_ref)
    high, low = cells_of(0, TILE_X, x_ref, iy_ref, wide_ref, rhs_ref)
    half = lax.axis_index("c")
    for part in range(4):
        lanes = slice(part * 256, (part + 1) * 256)
        table = depth_ref[half, 0, :, lanes]
        out_ref[:, lanes] = (
            dot(high, table)
            + dot(low, table)
            + dot(high, depth_ref[half, 1, :, lanes])
            + dot(slope_ref[:, lanes], l_ref[...])
        )


def expand_kernel(
    modes_ref,
    part_ref,
    depth_ref,
    x_ref,
    iy_ref,
    gw_ref,
    out_hbm,
    gw_hbm,
    wide_ref,
    rhs_ref,
    out_ref,
    sems,
    gw_sem,
):
    gw_copy = pltpu.make_async_copy(gw_ref, gw_hbm, gw_sem)
    gw_copy.start()
    turn_back(modes_ref, wide_ref)
    half = 1 - lax.axis_index("c")
    copies = [gw_copy]
    high, low = cells_of(0, TILE_X, x_ref, iy_ref, wide_ref, rhs_ref)
    for part in range(4):
        lanes = slice(part * 256, (part + 1) * 256)
        table = depth_ref[half, 0, :, lanes]
        out_ref[:, lanes] = (
            dot(high, table)
            + dot(low, table)
            + dot(high, depth_ref[half, 1, :, lanes])
            + part_ref[:, lanes]
        )
        copy = pltpu.make_async_copy(out_ref.at[:, lanes], out_hbm.at[:, lanes], sems.at[part])
        copy.start()
        copies.append(copy)
    for copy in copies:
        copy.wait()


def in_vmem(count):
    return [pl.BlockSpec(memory_space=pltpu.VMEM)] * count


IN_HBM = pl.BlockSpec(memory_space=pltpu.HBM)


def call(kernel, name, outs, ins, out_specs, scratch, flops=0):
    return pl.pallas_call(
        kernel,
        in_specs=ins,
        out_specs=out_specs,
        out_shape=[jax.ShapeDtypeStruct(*out) for out in outs],
        scratch_shapes=scratch,
        compiler_params=pltpu.CompilerParams(vmem_limit_bytes=20 * MIB),
        cost_estimate=pl.CostEstimate(flops=flops, bytes_accessed=4 * MIB, transcendentals=0),
        name=name,
    )


def in_hbm(value):
    return pltpu.with_memory_space_constraint(value, pltpu.HBM)


def on_device(cotangent, preact, spectra, spectral_weight, local_weight):
    table = {name: jnp.asarray(value) for name, value in tables().items()}
    swap = [(0, 1), (1, 0)]
    square = (ROWS, HALF)
    turn_scratch = pltpu.VMEM((6 * TILE_Y, TILE_X * QUARTER), BF16)
    cell_scratch = [pltpu.VMEM((CELLS, YS * QUARTER), BF16)] * 2

    slope, send = call(
        slope_kernel,
        "slope",
        [((ROWS, ROW), BF16), (square, F32)],
        [IN_HBM] * 2,
        in_vmem(2),
        [
            pltpu.VMEM((ROWS, ROW), BF16),
            pltpu.VMEM((ROWS, ROW), BF16),
            pltpu.VMEM((ROW, HALF), BF16),
            pltpu.SemaphoreType.DMA((2, CHUNKS)),
        ],
    )(in_hbm(cotangent.reshape(ROWS, ROW)), in_hbm(preact.reshape(ROWS, ROW)))
    depth = lax.ppermute(send, "c", swap)
    own, forward_x, inverse_x, local_map, forward_y, inverse_y = call(
        own_kernel,
        "own_cells",
        [
            ((BLOCK, YS * QUARTER), F32),
            ((2, 2, BLOCK, CELLS), BF16),
            ((2, CELLS, BLOCK), BF16),
            ((16 * CH, 16 * CH), BF16),
            ((2 * KY, 6 * TILE_Y), BF16),
            ((2 * TILE_Y, 6 * KY), BF16),
        ],
        in_vmem(2),
        in_vmem(6),
        [pltpu.VMEM((ROW, HALF), BF16), pltpu.VMEM(square, F32), turn_scratch, *cell_scratch],
        flops=2 * 10**9,
    )(slope, local_weight)
    (partial,) = call(
        modes_kernel,
        "modes",
        [((2048, QUARTER), BF16)],
        in_vmem(4),
        in_vmem(1),
        [turn_scratch, *cell_scratch],
    )(depth, own, forward_x, forward_y)
    partial = lax.all_to_all(partial.reshape(16, 128, QUARTER), PLANE, 0, 0, tiled=True, axis_index_groups=PLANE_ORDER)
    (sums,) = call(
        sum_kernel,
        "sums",
        [((128, QUARTER), BF16)],
        in_vmem(1),
        in_vmem(1),
        [],
    )(partial)
    sums = sums.reshape(32, 4, QUARTER)
    sums = lax.all_to_all(sums, LINE, 0, 0, tiled=True, axis_index_groups=LINE_ORDER)
    grad_weight, back = call(
        update_kernel,
        "update",
        [((2, 8192), F32), ((ZL * ZH, CS, 4, QUARTER), F32)],
        in_vmem(3),
        in_vmem(2),
        [],
    )(
        sums.reshape(ZL * ZH, CS, 4, QUARTER),
        spectra.reshape(2, 2 * HALF),
        spectral_weight.reshape(2, 8192),
    )
    back = lax.all_to_all(
        back.reshape(32, 4, QUARTER).astype(BF16),
        LINE,
        0,
        0,
        tiled=True,
        axis_index_groups=LINE_ORDER,
    )
    back = jnp.broadcast_to(back.reshape(1, 128, QUARTER), (16, 128, QUARTER))
    modes = lax.all_to_all(back, PLANE, 0, 0, tiled=True, axis_index_groups=PLANE_ORDER).reshape(2048, QUARTER)
    other = lax.ppermute(modes, "c", swap)
    back_scratch = [pltpu.VMEM((BLOCK, YS * QUARTER), BF16), turn_scratch]
    (part,) = call(
        expand_own_kernel,
        "expand_own",
        [((ROWS, ROW), F32)],
        in_vmem(6),
        in_vmem(1),
        back_scratch,
        flops=3 * 10**9,
    )(modes, slope, local_map, table["expand"], inverse_x, inverse_y)
    result, grad_weight = call(
        expand_kernel,
        "expand",
        [((ROWS, ROW), F32), ((2, 8192), F32)],
        in_vmem(6),
        [IN_HBM, IN_HBM],
        [
            *back_scratch,
            pltpu.VMEM((ROWS, ROW), F32),
            pltpu.SemaphoreType.DMA((4,)),
            pltpu.SemaphoreType.DMA,
        ],
    )(other, part, table["expand"], inverse_x, inverse_y, grad_weight)
    return result.reshape(TILE_X, TILE_Y, ROW), grad_weight.reshape(1, 2, 8192)


def solution(mesh):
    fine = Mesh(mesh.devices.reshape(ZL, XS, CS, ZH, YS), ("zl", "x", "c", "zh", "y"))
    split_spec = P(("zl", "x", "c"), ("zh", "y"), None)
    return jax.shard_map(
        on_device,
        mesh=fine,
        in_specs=(split_spec, split_spec, split_spec, split_spec, P()),
        out_specs=(split_spec, split_spec),
        check_vma=False,
    )
```

```python
import functools
import math

import jax
import jax.numpy as jnp
import ml_dtypes
import numpy as np
from jax import lax
from jax.experimental import pallas as pl
from jax.experimental.pallas import tpu as pltpu
from jax.sharding import Mesh
from jax.sharding import PartitionSpec as P

TILE_X, TILE_Y, DEPTH, CH = 16, 32, 64, 16
KX, KY, KZ = 32, 32, 16
NX, NY = 512, 512
ZL, XS, CS, ZH, YS = 4, 4, 2, 4, 4
ROW = DEPTH * CH
HALF = KZ * CH
QUARTER = 128
ROWS = TILE_X * TILE_Y
CHUNKS = 2
CHUNK_ROWS = ROWS // CHUNKS
NORM = 1.0 / math.sqrt(NX * NY * DEPTH)
F32, BF16 = jnp.float32, jnp.bfloat16
MIB = 1024 * 1024
PLANE = ("y", "x")
LINE = ("zl", "zh", "c")
FAR, FAR_PLANE = 2, 2
LINE_ORDER = [[(zl * ZH + (zh ^ FAR)) * CS + c for zl in range(ZL) for zh in range(ZH) for c in range(CS)]]
PLANE_ORDER = [[(y ^ FAR_PLANE) * XS + (x ^ FAR_PLANE) for y in range(YS) for x in range(XS)]]


def split_table(table):
    high = table.astype(ml_dtypes.bfloat16)
    low = (table - high.astype(np.float64)).astype(ml_dtypes.bfloat16)
    return high, low


@functools.cache
def tables():
    depth_angle = (np.outer(np.arange(DEPTH), np.arange(KZ)) % DEPTH) * (2.0 * np.pi / DEPTH)
    expand = np.stack([np.cos(depth_angle).T, -np.sin(depth_angle).T], 0) * NORM
    expand = expand.reshape(2, 2, 8, DEPTH).transpose(1, 0, 2, 3).reshape(2, KZ, DEPTH)
    expand = np.stack([np.kron(part, np.eye(CH)) for part in expand])
    expand = np.stack(split_table(expand), 1)
    return dict(
        expand=expand,
    )


def dot(left, right):
    return lax.dot_general(left, right, (((1,), (0,)), ((), ())), preferred_element_type=F32)


def dot_last(left, right):
    return lax.dot_general(left, right, (((1,), (1,)), ((), ())), preferred_element_type=F32)


def split(value):
    high = value.astype(BF16)
    return high, (value - high.astype(F32)).astype(BF16)


def store_split(ref, lanes, value):
    rows = value.shape[0]
    high, low = split(value)
    ref[:rows, lanes] = high
    ref[rows : 2 * rows, lanes] = low
    ref[2 * rows :, lanes] = high


def three_parts(value):
    high = value.astype(BF16)
    rest = value - high.astype(F32)
    middle = rest.astype(BF16)
    low = (rest - middle.astype(F32)).astype(BF16)
    return jnp.concatenate([high, middle, low], 0)


def sum_parts(value):
    rows = value.shape[0] // 3
    return value[:rows] + (value[rows : 2 * rows] + value[2 * rows :])


def gelu_slope(pre_value):
    normal_cdf = 0.5 * (1.0 + lax.erf(pre_value * (1.0 / math.sqrt(2.0))))
    return normal_cdf + pre_value * jnp.exp(-0.5 * pre_value * pre_value) * (
        1.0 / math.sqrt(2.0 * math.pi)
    )


def lanes_of(at):
    return slice(at * QUARTER, (at + 1) * QUARTER)


def iota(shape, axis):
    return lax.broadcasted_iota(jnp.int32, shape, axis)


def one_hot(condition):
    return condition.astype(F32).astype(BF16)


BLOCK, CELLS = 512, 256


def fill_forward(out_ref, small):
    shape = (128, 1024)
    cells = one_hot(iota(shape, 1) >> 3 == iota(shape, 0))
    shape = (128, 64)
    twice = one_hot(iota(shape, 0) >> 1 == iota(shape, 1))
    wide = dot(twice, dot(small, cells).astype(BF16))
    shape = (8, CELLS)
    local, ky = iota(shape, 0) & 1, iota(shape, 1) & 7
    masks = [(ky == 2 * zh + local).astype(F32) for zh in range(ZH)]
    for part in range(2):
        for source in range(2):
            first = (part * 2 + source) * CELLS
            for group in range(16):
                rows = wide[group * 8 : (group + 1) * 8, first : first + CELLS]
                rows = jnp.concatenate([rows * mask for mask in masks], 0).astype(BF16)
                out_ref[source, part, group * 32 : (group + 1) * 32, :] = rows


def fill_inverse(out_ref, small):
    shape = (64, BLOCK)
    row, column = iota(shape, 0), iota(shape, 1)
    modes = one_hot((column >> 5) * 4 + (column >> 1 & 3) == row)
    wide = lax.dot_general(small, modes, (((0,), (0,)), ((), ())), preferred_element_type=F32)
    shape = (8, BLOCK)
    row, column = iota(shape, 0), iota(shape, 1)
    mask = ((column >> 3 & 3) * 2 + (column & 1) == row).astype(F32)
    for part in range(2):
        for cell in range(TILE_X):
            at = part * 64 + cell * 2
            rows = [jnp.broadcast_to(wide[i : i + 1], shape) * mask for i in (at, at + 1)]
            out_ref[part, cell * 16 : (cell + 1) * 16, :] = jnp.concatenate(rows, 0).astype(BF16)


def fill_local(out_ref, local_ref):
    shape = (16 * CH, CH)
    pick = one_hot((iota(shape, 0) & (CH - 1)) == iota(shape, 1))
    full = dot_last(dot_last(pick, local_ref[...]).astype(BF16), pick)
    shape = (16 * CH, 16 * CH)
    same = iota(shape, 0) >> 4 == iota(shape, 1) >> 4
    out_ref[...] = jnp.where(same, full, 0.0).astype(BF16)


def turn(units):
    distance = jnp.abs((units + 256 & 511) - 256)
    far = distance > 128
    near = jnp.where(far, 256 - distance, distance)
    square = near.astype(F32) * (2.0 * math.pi / 512)
    square = square * square
    value = jnp.full(units.shape, 1.0 / math.factorial(12), F32)
    for power in (10, 8, 6, 4, 2, 0):
        value = value * square + (-1.0) ** (power // 2) / math.factorial(power)
    value = jnp.where(near == 128, 0.0, value)
    return jnp.where(far, -value, value)


def mode_of(ordinal):
    return jnp.where(ordinal < 16, ordinal, ordinal - 32)


def x_table(tile):
    shape = (2 * KX, 8 * TILE_X)
    row, column = iota(shape, 0), iota(shape, 1)
    mode = mode_of((row >> 2 & 3) * 8 + ((row >> 4) ^ FAR_PLANE) * 2 + (row >> 1 & 1))
    cell = (tile ^ (column >> 5 & 1)) * TILE_X + (column >> 1 & 15)
    value = turn(mode * cell + 128 * ((row & 1) - (column & 1)))
    high = value.astype(BF16)
    low = (value - high.astype(F32)).astype(BF16)
    return jnp.where(column < 4 * TILE_X, high.astype(F32), low.astype(F32)).astype(BF16)


def y_table(tile, inverse):
    shape = (64, 192)
    mode, cell = iota(shape, 0), iota(shape, 1)
    column = cell
    if inverse:
        mode, cell = cell, mode
    ordinal = ((mode >> 1 & 3) ^ FAR) * 8 + ((mode >> 4 & 3) ^ FAR_PLANE) * 2 + (mode & 1)
    place = tile * TILE_Y + (cell & 31)
    value = turn(mode_of(ordinal) * place + 128 * ((mode >> 3 & 1) - (cell >> 5 & 1)))
    high = value.astype(BF16)
    low = (value - high.astype(F32)).astype(BF16)
    return jnp.where(column < 128, high.astype(F32), low.astype(F32)).astype(BF16)


def fill_project(f_ref, half):
    shape = (DEPTH, HALF)
    z, column = iota(shape, 0), iota(shape, 1)
    kz = half * 8 + (column >> 4 & 7)
    factor = turn((kz * z & 63) * 8 + 128 * (column >> 7))
    factor = jnp.where(kz == 0, factor, 2.0 * factor)
    shape = (CH, HALF)
    same = iota(shape, 0) == (iota(shape, 1) & (CH - 1))
    for z in range(DEPTH):
        rows = jnp.broadcast_to(factor[z : z + 1], shape)
        f_ref[z * CH : (z + 1) * CH, :] = jnp.where(same, rows, 0.0).astype(BF16)


def place_of():
    core = lax.axis_index("c")
    x_tile = (lax.axis_index("zl") * XS + lax.axis_index("x")) * CS + core
    return x_tile, lax.axis_index("zh") * YS + lax.axis_index("y"), core


def slope_kernel(cot_hbm, pre_hbm, slope_ref, send_ref, cot_ref, pre_ref, f_ref, sems):
    def copies(chunk):
        rows = pl.ds(chunk * CHUNK_ROWS, CHUNK_ROWS)
        return (
            pltpu.make_async_copy(cot_hbm.at[rows], cot_ref.at[rows], sems.at[0, chunk]),
            pltpu.make_async_copy(pre_hbm.at[rows], pre_ref.at[rows], sems.at[1, chunk]),
        )

    for chunk in range(CHUNKS):
        for copy in copies(chunk):
            copy.start()
    fill_project(f_ref, 1 - lax.axis_index("c"))
    for chunk in range(CHUNKS):
        for copy in copies(chunk):
            copy.wait()
        rows = slice(chunk * CHUNK_ROWS, (chunk + 1) * CHUNK_ROWS)
        pre_value = pre_ref[rows, :].astype(F32)
        slope = (cot_ref[rows, :].astype(F32) * gelu_slope(pre_value)).astype(BF16)
        slope_ref[rows, :] = slope
    send_ref[...] = dot(slope_ref[...], f_ref[...])


def turn_y(depth, fy_ref, rhs_ref, high_ref, low_ref):
    for x in range(TILE_X):
        block = depth[x * TILE_Y : (x + 1) * TILE_Y]
        stacked = jnp.concatenate([block[:, :QUARTER], block[:, QUARTER:]], 0)
        store_split(rhs_ref, lanes_of(x), stacked)
    turned = dot(fy_ref[...], rhs_ref[...])
    for x in range(TILE_X):
        for y in range(YS):
            high, low = split(turned[y * 16 : (y + 1) * 16, lanes_of(x)])
            high_ref[x * 16 : (x + 1) * 16, lanes_of(y)] = high
            low_ref[x * 16 : (x + 1) * 16, lanes_of(y)] = low


def turn_x(table_high, table_low, high, low):
    return dot(table_high, high) + dot(table_high, low) + dot(table_low, high)


def own_kernel(
    slope_ref,
    local_ref,
    part_ref,
    forward_ref,
    inverse_ref,
    l_ref,
    fy_ref,
    iy_ref,
    f_ref,
    depth_ref,
    rhs_ref,
    high_ref,
    low_ref,
):
    x_tile, y_tile, core = place_of()
    fill_project(f_ref, core)
    for chunk in range(4):
        rows = slice(chunk * ROWS // 4, (chunk + 1) * ROWS // 4)
        depth_ref[rows, :] = dot(slope_ref[rows, :], f_ref[...])
    fy_ref[...] = y_table(y_tile, False)
    iy_ref[...] = y_table(y_tile, True)
    small = x_table(x_tile)
    fill_forward(forward_ref, small)
    fill_inverse(inverse_ref, small)
    fill_local(l_ref, local_ref)
    turn_y(depth_ref[...], fy_ref, rhs_ref, high_ref, low_ref)
    for part in range(2):
        lanes = slice(part * 256, (part + 1) * 256)
        part_ref[:, lanes] = turn_x(
            forward_ref[0, 0], forward_ref[0, 1], high_ref[:, lanes], low_ref[:, lanes]
        )


def modes_kernel(depth_ref, part_ref, x_ref, fy_ref, out_ref, rhs_ref, high_ref, low_ref):
    turn_y(depth_ref[...], fy_ref, rhs_ref, high_ref, low_ref)
    turned = part_ref[...] + turn_x(x_ref[1, 0], x_ref[1, 1], high_ref[...], low_ref[...])
    for y in range(YS):
        out_ref[y * BLOCK : (y + 1) * BLOCK, :] = turned[:, lanes_of(y)].astype(BF16)


def sum_kernel(part_ref, out_ref):
    out_ref[...] = jnp.sum(part_ref[...].astype(F32), 0).astype(BF16)


def update_kernel(sum_ref, spectra_ref, weight_ref, gw_ref, sg_ref):
    halves = [jnp.sum(sum_ref[:, half].astype(F32), 0) * NORM for half in range(2)]
    grad = jnp.concatenate([halves[0][:2], halves[1][:2], halves[0][2:], halves[1][2:]], 0)
    saved = jnp.concatenate([spectra_ref[:, b * 128 : (b + 1) * 128] for b in range(4)], 0)
    shape = (64, QUARTER)
    own_kz = iota(shape, 0) >> 3 == iota(shape, 1) >> 4
    shape = (QUARTER, CH * CH)
    row, column = iota(shape, 0) & (CH - 1), iota(shape, 1)
    spread_c = one_hot(row == column >> 4)
    spread_o = one_hot(row == (column & (CH - 1)))

    def spread(value, table):
        rows = jnp.where(own_kz, jnp.concatenate([value] * 8, 0), 0.0)
        return sum_parts(dot(three_parts(rows), table))

    grad_wide, saved_wide = spread(grad, spread_o), spread(saved, spread_c)
    weight = jnp.concatenate(
        [
            weight_ref[:, b * 2048 + kz * 256 : b * 2048 + (kz + 1) * 256]
            for kz in range(8)
            for b in range(4)
        ],
        0,
    )
    real_rows = (iota((64, CH * CH), 0) & 4) == 0

    def combine(value):
        product = value * grad_wide
        crossed = swap_parts(value) * grad_wide
        return jnp.where(
            real_rows, product + swap_parts(product), crossed - swap_parts(crossed)
        )

    def swap_parts(value):
        return jnp.where(real_rows, pltpu.roll(value, 60, 0), pltpu.roll(value, 4, 0))

    outer = combine(saved_wide)
    for kz in range(8):
        for b in range(4):
            lanes = slice(b * 2048 + kz * 256, b * 2048 + (kz + 1) * 256)
            gw_ref[:, lanes] = outer[kz * 8 + b * 2 : kz * 8 + b * 2 + 2]
    back = sum_parts(dot_last(three_parts(combine(weight)), spread_c))
    back = jnp.where(own_kz, back, 0.0)
    back = functools.reduce(jnp.add, [back[kz * 8 : (kz + 1) * 8] for kz in range(8)])
    back = back.astype(BF16).astype(F32)
    for half in range(2):
        rows = jnp.concatenate([back[2 * half : 2 * half + 2], back[2 * half + 4 : 2 * half + 6]], 0)
        sg_ref[:, half] = jnp.broadcast_to(rows[None], (ZL * ZH, 4, QUARTER))


def turn_back(modes_ref, wide_ref):
    for y in range(YS):
        wide_ref[:, lanes_of(y)] = modes_ref[y * BLOCK : (y + 1) * BLOCK, :]


def cells_of(first, count, x_ref, iy_ref, wide_ref, rhs_ref):
    rows = slice(first * 16, (first + count) * 16)
    turned = dot(x_ref[0, rows, :], wide_ref[...]) + dot(x_ref[1, rows, :], wide_ref[...])
    for x in range(count):
        for y in range(YS):
            high, low = split(turned[x * 16 : (x + 1) * 16, lanes_of(y)])
            for at, part in enumerate((high, low, high)):
                rows = slice(at * 2 * KY + y * 16, at * 2 * KY + (y + 1) * 16)
                rhs_ref[rows, lanes_of(first + x)] = part
    turned = dot(iy_ref[...], rhs_ref[:, first * QUARTER : (first + count) * QUARTER])
    cells = [
        jnp.concatenate([turned[:TILE_Y, lanes_of(x)], turned[TILE_Y:, lanes_of(x)]], 1)
        for x in range(count)
    ]
    return split(jnp.concatenate(cells, 0))


def expand_own_kernel(
    modes_ref, slope_ref, l_ref, depth_ref, x_ref, iy_ref, out_ref, wide_ref, rhs_ref
):
    turn_back(modes_ref, wide_ref)
    high, low = cells_of(0, TILE_X, x_ref, iy_ref, wide_ref, rhs_ref)
    half = lax.axis_index("c")
    for part in range(4):
        lanes = slice(part * 256, (part + 1) * 256)
        table = depth_ref[half, 0, :, lanes]
        out_ref[:, lanes] = (
            dot(high, table)
            + dot(low, table)
            + dot(high, depth_ref[half, 1, :, lanes])
            + dot(slope_ref[:, lanes], l_ref[...])
        )


def expand_kernel(
    modes_ref,
    part_ref,
    depth_ref,
    x_ref,
    iy_ref,
    gw_ref,
    out_hbm,
    gw_hbm,
    wide_ref,
    rhs_ref,
    out_ref,
    sems,
    gw_sem,
):
    gw_copy = pltpu.make_async_copy(gw_ref, gw_hbm, gw_sem)
    gw_copy.start()
    turn_back(modes_ref, wide_ref)
    half = 1 - lax.axis_index("c")
    copies = [gw_copy]
    high, low = cells_of(0, TILE_X, x_ref, iy_ref, wide_ref, rhs_ref)
    for part in range(4):
        lanes = slice(part * 256, (part + 1) * 256)
        table = depth_ref[half, 0, :, lanes]
        out_ref[:, lanes] = (
            dot(high, table)
            + dot(low, table)
            + dot(high, depth_ref[half, 1, :, lanes])
            + part_ref[:, lanes]
        )
        copy = pltpu.make_async_copy(out_ref.at[:, lanes], out_hbm.at[:, lanes], sems.at[part])
        copy.start()
        copies.append(copy)
    for copy in copies:
        copy.wait()


def in_vmem(count):
    return [pl.BlockSpec(memory_space=pltpu.VMEM)] * count


IN_HBM = pl.BlockSpec(memory_space=pltpu.HBM)


def call(kernel, name, outs, ins, out_specs, scratch, flops=0):
    return pl.pallas_call(
        kernel,
        in_specs=ins,
        out_specs=out_specs,
        out_shape=[jax.ShapeDtypeStruct(*out) for out in outs],
        scratch_shapes=scratch,
        compiler_params=pltpu.CompilerParams(vmem_limit_bytes=20 * MIB),
        cost_estimate=pl.CostEstimate(flops=flops, bytes_accessed=4 * MIB, transcendentals=0),
        name=name,
    )


def in_hbm(value):
    return pltpu.with_memory_space_constraint(value, pltpu.HBM)


def on_device(cotangent, preact, spectra, spectral_weight, local_weight):
    table = {name: jnp.asarray(value) for name, value in tables().items()}
    swap = [(0, 1), (1, 0)]
    square = (ROWS, HALF)
    turn_scratch = pltpu.VMEM((6 * TILE_Y, TILE_X * QUARTER), BF16)
    cell_scratch = [pltpu.VMEM((CELLS, YS * QUARTER), BF16)] * 2

    slope, send = call(
        slope_kernel,
        "slope",
        [((ROWS, ROW), BF16), (square, F32)],
        [IN_HBM] * 2,
        in_vmem(2),
        [
            pltpu.VMEM((ROWS, ROW), BF16),
            pltpu.VMEM((ROWS, ROW), BF16),
            pltpu.VMEM((ROW, HALF), BF16),
            pltpu.SemaphoreType.DMA((2, CHUNKS)),
        ],
    )(in_hbm(cotangent.reshape(ROWS, ROW)), in_hbm(preact.reshape(ROWS, ROW)))
    depth = lax.ppermute(send, "c", swap)
    own, forward_x, inverse_x, local_map, forward_y, inverse_y = call(
        own_kernel,
        "own_cells",
        [
            ((BLOCK, YS * QUARTER), F32),
            ((2, 2, BLOCK, CELLS), BF16),
            ((2, CELLS, BLOCK), BF16),
            ((16 * CH, 16 * CH), BF16),
            ((2 * KY, 6 * TILE_Y), BF16),
            ((2 * TILE_Y, 6 * KY), BF16),
        ],
        in_vmem(2),
        in_vmem(6),
        [pltpu.VMEM((ROW, HALF), BF16), pltpu.VMEM(square, F32), turn_scratch, *cell_scratch],
        flops=2 * 10**9,
    )(slope, local_weight)
    (partial,) = call(
        modes_kernel,
        "modes",
        [((2048, QUARTER), BF16)],
        in_vmem(4),
        in_vmem(1),
        [turn_scratch, *cell_scratch],
    )(depth, own, forward_x, forward_y)
    partial = lax.all_to_all(partial.reshape(16, 128, QUARTER), PLANE, 0, 0, tiled=True, axis_index_groups=PLANE_ORDER)
    (sums,) = call(
        sum_kernel,
        "sums",
        [((128, QUARTER), BF16)],
        in_vmem(1),
        in_vmem(1),
        [],
    )(partial)
    sums = sums.reshape(32, 4, QUARTER)
    sums = lax.all_to_all(sums, LINE, 0, 0, tiled=True, axis_index_groups=LINE_ORDER)
    grad_weight, back = call(
        update_kernel,
        "update",
        [((2, 8192), F32), ((ZL * ZH, CS, 4, QUARTER), F32)],
        in_vmem(3),
        in_vmem(2),
        [],
    )(
        sums.reshape(ZL * ZH, CS, 4, QUARTER),
        spectra.reshape(2, 2 * HALF),
        spectral_weight.reshape(2, 8192),
    )
    back = lax.all_to_all(
        back.reshape(32, 4, QUARTER).astype(BF16),
        LINE,
        0,
        0,
        tiled=True,
        axis_index_groups=LINE_ORDER,
    )
    back = jnp.broadcast_to(back.reshape(1, 128, QUARTER), (16, 128, QUARTER))
    modes = lax.all_to_all(back, PLANE, 0, 0, tiled=True, axis_index_groups=PLANE_ORDER).reshape(2048, QUARTER)
    other = lax.ppermute(modes, "c", swap)
    back_scratch = [pltpu.VMEM((BLOCK, YS * QUARTER), BF16), turn_scratch]
    (part,) = call(
        expand_own_kernel,
        "expand_own",
        [((ROWS, ROW), F32)],
        in_vmem(6),
        in_vmem(1),
        back_scratch,
        flops=3 * 10**9,
    )(modes, slope, local_map, table["expand"], inverse_x, inverse_y)
    result, grad_weight = call(
        expand_kernel,
        "expand",
        [((ROWS, ROW), F32), ((2, 8192), F32)],
        in_vmem(6),
        [IN_HBM, IN_HBM],
        [
            *back_scratch,
            pltpu.VMEM((ROWS, ROW), F32),
            pltpu.SemaphoreType.DMA((4,)),
            pltpu.SemaphoreType.DMA,
        ],
    )(other, part, table["expand"], inverse_x, inverse_y, grad_weight)
    return result.reshape(TILE_X, TILE_Y, ROW), grad_weight.reshape(1, 2, 8192)


def solution(mesh):
    fine = Mesh(mesh.devices.reshape(ZL, XS, CS, ZH, YS), ("zl", "x", "c", "zh", "y"))
    split_spec = P(("zl", "x", "c"), ("zh", "y"), None)
    return jax.shard_map(
        on_device,
        mesh=fine,
        in_specs=(split_spec, split_spec, split_spec, split_spec, P()),
        out_specs=(split_spec, split_spec),
        check_vma=False,
    )
```

```python
import functools
import math

import jax
import jax.numpy as jnp
import ml_dtypes
import numpy as np
from jax import lax
from jax.experimental import pallas as pl
from jax.experimental.pallas import tpu as pltpu
from jax.sharding import Mesh
from jax.sharding import PartitionSpec as P

TILE_X, TILE_Y, DEPTH, CH = 16, 32, 64, 16
KX, KY, KZ = 32, 32, 16
NX, NY = 512, 512
ZL, XS, CS, ZH, YS = 4, 4, 2, 4, 4
ROW = DEPTH * CH
HALF = KZ * CH
QUARTER = 128
ROWS = TILE_X * TILE_Y
CHUNKS = 2
CHUNK_ROWS = ROWS // CHUNKS
NORM = 1.0 / math.sqrt(NX * NY * DEPTH)
F32, BF16 = jnp.float32, jnp.bfloat16
MIB = 1024 * 1024
PLANE = ("y", "x")
LINE = ("zl", "zh", "c")
FAR, FAR_PLANE = 2, 2
LINE_ORDER = [[((zl ^ 1) * ZH + (zh ^ FAR)) * CS + c for zl in range(ZL) for zh in range(ZH) for c in range(CS)]]
PLANE_ORDER = [[(y ^ FAR_PLANE) * XS + (x ^ FAR_PLANE) for y in range(YS) for x in range(XS)]]


def split_table(table):
    high = table.astype(ml_dtypes.bfloat16)
    low = (table - high.astype(np.float64)).astype(ml_dtypes.bfloat16)
    return high, low


@functools.cache
def tables():
    depth_angle = (np.outer(np.arange(DEPTH), np.arange(KZ)) % DEPTH) * (2.0 * np.pi / DEPTH)
    expand = np.stack([np.cos(depth_angle).T, -np.sin(depth_angle).T], 0) * NORM
    expand = expand.reshape(2, 2, 8, DEPTH).transpose(1, 0, 2, 3).reshape(2, KZ, DEPTH)
    expand = np.stack([np.kron(part, np.eye(CH)) for part in expand])
    expand = np.stack(split_table(expand), 1)
    return dict(
        expand=expand,
    )


def dot(left, right):
    return lax.dot_general(left, right, (((1,), (0,)), ((), ())), preferred_element_type=F32)


def dot_last(left, right):
    return lax.dot_general(left, right, (((1,), (1,)), ((), ())), preferred_element_type=F32)


def split(value):
    high = value.astype(BF16)
    return high, (value - high.astype(F32)).astype(BF16)


def store_split(ref, lanes, value):
    rows = value.shape[0]
    high, low = split(value)
    ref[:rows, lanes] = high
    ref[rows : 2 * rows, lanes] = low
    ref[2 * rows :, lanes] = high


def three_parts(value):
    high = value.astype(BF16)
    rest = value - high.astype(F32)
    middle = rest.astype(BF16)
    low = (rest - middle.astype(F32)).astype(BF16)
    return jnp.concatenate([high, middle, low], 0)


def sum_parts(value):
    rows = value.shape[0] // 3
    return value[:rows] + (value[rows : 2 * rows] + value[2 * rows :])


def gelu_slope(pre_value):
    normal_cdf = 0.5 * (1.0 + lax.erf(pre_value * (1.0 / math.sqrt(2.0))))
    return normal_cdf + pre_value * jnp.exp(-0.5 * pre_value * pre_value) * (
        1.0 / math.sqrt(2.0 * math.pi)
    )


def lanes_of(at):
    return slice(at * QUARTER, (at + 1) * QUARTER)


def iota(shape, axis):
    return lax.broadcasted_iota(jnp.int32, shape, axis)


def one_hot(condition):
    return condition.astype(F32).astype(BF16)


BLOCK, CELLS = 512, 256


def fill_forward(out_ref, small):
    shape = (128, 1024)
    cells = one_hot(iota(shape, 1) >> 3 == iota(shape, 0))
    shape = (128, 64)
    twice = one_hot(iota(shape, 0) >> 1 == iota(shape, 1))
    wide = dot(twice, dot(small, cells).astype(BF16))
    shape = (8, CELLS)
    local, ky = iota(shape, 0) & 1, iota(shape, 1) & 7
    masks = [(ky == 2 * zh + local).astype(F32) for zh in range(ZH)]
    for part in range(2):
        for source in range(2):
            first = (part * 2 + source) * CELLS
            for group in range(16):
                rows = wide[group * 8 : (group + 1) * 8, first : first + CELLS]
                rows = jnp.concatenate([rows * mask for mask in masks], 0).astype(BF16)
                out_ref[source, part, group * 32 : (group + 1) * 32, :] = rows


def fill_inverse(out_ref, small):
    shape = (64, BLOCK)
    row, column = iota(shape, 0), iota(shape, 1)
    modes = one_hot((column >> 5) * 4 + (column >> 1 & 3) == row)
    wide = lax.dot_general(small, modes, (((0,), (0,)), ((), ())), preferred_element_type=F32)
    shape = (8, BLOCK)
    row, column = iota(shape, 0), iota(shape, 1)
    mask = ((column >> 3 & 3) * 2 + (column & 1) == row).astype(F32)
    for part in range(2):
        for cell in range(TILE_X):
            at = part * 64 + cell * 2
            rows = [jnp.broadcast_to(wide[i : i + 1], shape) * mask for i in (at, at + 1)]
            out_ref[part, cell * 16 : (cell + 1) * 16, :] = jnp.concatenate(rows, 0).astype(BF16)


def fill_local(out_ref, local_ref):
    shape = (16 * CH, CH)
    pick = one_hot((iota(shape, 0) & (CH - 1)) == iota(shape, 1))
    full = dot_last(dot_last(pick, local_ref[...]).astype(BF16), pick)
    shape = (16 * CH, 16 * CH)
    same = iota(shape, 0) >> 4 == iota(shape, 1) >> 4
    out_ref[...] = jnp.where(same, full, 0.0).astype(BF16)


def turn(units):
    distance = jnp.abs((units + 256 & 511) - 256)
    far = distance > 128
    near = jnp.where(far, 256 - distance, distance)
    square = near.astype(F32) * (2.0 * math.pi / 512)
    square = square * square
    value = jnp.full(units.shape, 1.0 / math.factorial(12), F32)
    for power in (10, 8, 6, 4, 2, 0):
        value = value * square + (-1.0) ** (power // 2) / math.factorial(power)
    value = jnp.where(near == 128, 0.0, value)
    return jnp.where(far, -value, value)


def mode_of(ordinal):
    return jnp.where(ordinal < 16, ordinal, ordinal - 32)


def x_table(tile):
    shape = (2 * KX, 8 * TILE_X)
    row, column = iota(shape, 0), iota(shape, 1)
    mode = mode_of(((row >> 2 & 3) ^ 1) * 8 + ((row >> 4) ^ FAR_PLANE) * 2 + (row >> 1 & 1))
    cell = (tile ^ (column >> 5 & 1)) * TILE_X + (column >> 1 & 15)
    value = turn(mode * cell + 128 * ((row & 1) - (column & 1)))
    high = value.astype(BF16)
    low = (value - high.astype(F32)).astype(BF16)
    return jnp.where(column < 4 * TILE_X, high.astype(F32), low.astype(F32)).astype(BF16)


def y_table(tile, inverse):
    shape = (64, 192)
    mode, cell = iota(shape, 0), iota(shape, 1)
    column = cell
    if inverse:
        mode, cell = cell, mode
    ordinal = ((mode >> 1 & 3) ^ FAR) * 8 + ((mode >> 4 & 3) ^ FAR_PLANE) * 2 + (mode & 1)
    place = tile * TILE_Y + (cell & 31)
    value = turn(mode_of(ordinal) * place + 128 * ((mode >> 3 & 1) - (cell >> 5 & 1)))
    high = value.astype(BF16)
    low = (value - high.astype(F32)).astype(BF16)
    return jnp.where(column < 128, high.astype(F32), low.astype(F32)).astype(BF16)


def fill_project(f_ref, half):
    shape = (DEPTH, HALF)
    z, column = iota(shape, 0), iota(shape, 1)
    kz = half * 8 + (column >> 4 & 7)
    factor = turn((kz * z & 63) * 8 + 128 * (column >> 7))
    factor = jnp.where(kz == 0, factor, 2.0 * factor)
    shape = (CH, HALF)
    same = iota(shape, 0) == (iota(shape, 1) & (CH - 1))
    for z in range(DEPTH):
        rows = jnp.broadcast_to(factor[z : z + 1], shape)
        f_ref[z * CH : (z + 1) * CH, :] = jnp.where(same, rows, 0.0).astype(BF16)


def place_of():
    core = lax.axis_index("c")
    x_tile = (lax.axis_index("zl") * XS + lax.axis_index("x")) * CS + core
    return x_tile, lax.axis_index("zh") * YS + lax.axis_index("y"), core


def slope_kernel(cot_hbm, pre_hbm, slope_ref, send_ref, cot_ref, pre_ref, f_ref, sems):
    def copies(chunk):
        rows = pl.ds(chunk * CHUNK_ROWS, CHUNK_ROWS)
        return (
            pltpu.make_async_copy(cot_hbm.at[rows], cot_ref.at[rows], sems.at[0, chunk]),
            pltpu.make_async_copy(pre_hbm.at[rows], pre_ref.at[rows], sems.at[1, chunk]),
        )

    for chunk in range(CHUNKS):
        for copy in copies(chunk):
            copy.start()
    fill_project(f_ref, 1 - lax.axis_index("c"))
    for chunk in range(CHUNKS):
        for copy in copies(chunk):
            copy.wait()
        rows = slice(chunk * CHUNK_ROWS, (chunk + 1) * CHUNK_ROWS)
        pre_value = pre_ref[rows, :].astype(F32)
        slope = (cot_ref[rows, :].astype(F32) * gelu_slope(pre_value)).astype(BF16)
        slope_ref[rows, :] = slope
        send_ref[rows, :] = dot(slope_ref[rows, :], f_ref[...])


def turn_y(depth, fy_ref, rhs_ref, high_ref, low_ref):
    for x in range(TILE_X):
        block = depth[x * TILE_Y : (x + 1) * TILE_Y]
        stacked = jnp.concatenate([block[:, :QUARTER], block[:, QUARTER:]], 0)
        store_split(rhs_ref, lanes_of(x), stacked)
    turned = dot(fy_ref[...], rhs_ref[...])
    for x in range(TILE_X):
        for y in range(YS):
            high, low = split(turned[y * 16 : (y + 1) * 16, lanes_of(x)])
            high_ref[x * 16 : (x + 1) * 16, lanes_of(y)] = high
            low_ref[x * 16 : (x + 1) * 16, lanes_of(y)] = low


def turn_x(table_high, table_low, high, low):
    return dot(table_high, high) + dot(table_high, low) + dot(table_low, high)


def own_kernel(
    slope_ref,
    local_ref,
    part_ref,
    forward_ref,
    inverse_ref,
    l_ref,
    fy_ref,
    iy_ref,
    f_ref,
    depth_ref,
    rhs_ref,
    high_ref,
    low_ref,
):
    x_tile, y_tile, core = place_of()
    fill_project(f_ref, core)
    for chunk in range(4):
        rows = slice(chunk * ROWS // 4, (chunk + 1) * ROWS // 4)
        depth_ref[rows, :] = dot(slope_ref[rows, :], f_ref[...])
    fy_ref[...] = y_table(y_tile, False)
    iy_ref[...] = y_table(y_tile, True)
    small = x_table(x_tile)
    fill_forward(forward_ref, small)
    fill_inverse(inverse_ref, small)
    fill_local(l_ref, local_ref)
    turn_y(depth_ref[...], fy_ref, rhs_ref, high_ref, low_ref)
    for part in range(2):
        lanes = slice(part * 256, (part + 1) * 256)
        part_ref[:, lanes] = turn_x(
            forward_ref[0, 0], forward_ref[0, 1], high_ref[:, lanes], low_ref[:, lanes]
        )


def modes_kernel(depth_ref, part_ref, x_ref, fy_ref, out_ref, rhs_ref, high_ref, low_ref):
    turn_y(depth_ref[...], fy_ref, rhs_ref, high_ref, low_ref)
    turned = part_ref[...] + turn_x(x_ref[1, 0], x_ref[1, 1], high_ref[...], low_ref[...])
    for y in range(YS):
        out_ref[y * BLOCK : (y + 1) * BLOCK, :] = turned[:, lanes_of(y)].astype(BF16)


def sum_kernel(part_ref, out_ref):
    out_ref[...] = jnp.sum(part_ref[...].astype(F32), 0).astype(BF16)


def update_kernel(sum_ref, spectra_ref, weight_ref, gw_ref, sg_ref):
    halves = [jnp.sum(sum_ref[:, half].astype(F32), 0) * NORM for half in range(2)]
    grad = jnp.concatenate([halves[0][:2], halves[1][:2], halves[0][2:], halves[1][2:]], 0)
    saved = jnp.concatenate([spectra_ref[:, b * 128 : (b + 1) * 128] for b in range(4)], 0)
    shape = (64, QUARTER)
    own_kz = iota(shape, 0) >> 3 == iota(shape, 1) >> 4
    shape = (QUARTER, CH * CH)
    row, column = iota(shape, 0) & (CH - 1), iota(shape, 1)
    spread_c = one_hot(row == column >> 4)
    spread_o = one_hot(row == (column & (CH - 1)))

    def spread(value, table):
        rows = jnp.where(own_kz, jnp.concatenate([value] * 8, 0), 0.0)
        return sum_parts(dot(three_parts(rows), table))

    grad_wide, saved_wide = spread(grad, spread_o), spread(saved, spread_c)
    weight = jnp.concatenate(
        [
            weight_ref[:, b * 2048 + kz * 256 : b * 2048 + (kz + 1) * 256]
            for kz in range(8)
            for b in range(4)
        ],
        0,
    )
    real_rows = (iota((64, CH * CH), 0) & 4) == 0

    def combine(value):
        product = value * grad_wide
        crossed = swap_parts(value) * grad_wide
        return jnp.where(
            real_rows, product + swap_parts(product), crossed - swap_parts(crossed)
        )

    def swap_parts(value):
        return jnp.where(real_rows, pltpu.roll(value, 60, 0), pltpu.roll(value, 4, 0))

    outer = combine(saved_wide)
    for kz in range(8):
        for b in range(4):
            lanes = slice(b * 2048 + kz * 256, b * 2048 + (kz + 1) * 256)
            gw_ref[:, lanes] = outer[kz * 8 + b * 2 : kz * 8 + b * 2 + 2]
    back = sum_parts(dot_last(three_parts(combine(weight)), spread_c))
    back = jnp.where(own_kz, back, 0.0)
    back = functools.reduce(jnp.add, [back[kz * 8 : (kz + 1) * 8] for kz in range(8)])
    back = back.astype(BF16).astype(F32)
    for half in range(2):
        rows = jnp.concatenate([back[2 * half : 2 * half + 2], back[2 * half + 4 : 2 * half + 6]], 0)
        sg_ref[:, half] = jnp.broadcast_to(rows[None], (ZL * ZH, 4, QUARTER))


def turn_back(modes_ref, wide_ref):
    for y in range(YS):
        wide_ref[:, lanes_of(y)] = modes_ref[y * BLOCK : (y + 1) * BLOCK, :]


def cells_of(first, count, x_ref, iy_ref, wide_ref, rhs_ref):
    rows = slice(first * 16, (first + count) * 16)
    turned = dot(x_ref[0, rows, :], wide_ref[...]) + dot(x_ref[1, rows, :], wide_ref[...])
    for x in range(count):
        for y in range(YS):
            high, low = split(turned[x * 16 : (x + 1) * 16, lanes_of(y)])
            for at, part in enumerate((high, low, high)):
                rows = slice(at * 2 * KY + y * 16, at * 2 * KY + (y + 1) * 16)
                rhs_ref[rows, lanes_of(first + x)] = part
    turned = dot(iy_ref[...], rhs_ref[:, first * QUARTER : (first + count) * QUARTER])
    cells = [
        jnp.concatenate([turned[:TILE_Y, lanes_of(x)], turned[TILE_Y:, lanes_of(x)]], 1)
        for x in range(count)
    ]
    return split(jnp.concatenate(cells, 0))


def expand_own_kernel(
    modes_ref, slope_ref, l_ref, depth_ref, x_ref, iy_ref, out_ref, wide_ref, rhs_ref
):
    turn_back(modes_ref, wide_ref)
    high, low = cells_of(0, TILE_X, x_ref, iy_ref, wide_ref, rhs_ref)
    half = lax.axis_index("c")
    for part in range(4):
        lanes = slice(part * 256, (part + 1) * 256)
        table = depth_ref[half, 0, :, lanes]
        out_ref[:, lanes] = (
            dot(high, table)
            + dot(low, table)
            + dot(high, depth_ref[half, 1, :, lanes])
            + dot(slope_ref[:, lanes], l_ref[...])
        )


def expand_kernel(
    modes_ref,
    part_ref,
    depth_ref,
    x_ref,
    iy_ref,
    gw_ref,
    out_hbm,
    gw_hbm,
    wide_ref,
    rhs_ref,
    out_ref,
    sems,
    gw_sem,
):
    gw_copy = pltpu.make_async_copy(gw_ref, gw_hbm, gw_sem)
    gw_copy.start()
    turn_back(modes_ref, wide_ref)
    half = 1 - lax.axis_index("c")
    copies = [gw_copy]
    high, low = cells_of(0, TILE_X, x_ref, iy_ref, wide_ref, rhs_ref)
    for part in range(4):
        lanes = slice(part * 256, (part + 1) * 256)
        table = depth_ref[half, 0, :, lanes]
        out_ref[:, lanes] = (
            dot(high, table)
            + dot(low, table)
            + dot(high, depth_ref[half, 1, :, lanes])
            + part_ref[:, lanes]
        )
        copy = pltpu.make_async_copy(out_ref.at[:, lanes], out_hbm.at[:, lanes], sems.at[part])
        copy.start()
        copies.append(copy)
    for copy in copies:
        copy.wait()


def in_vmem(count):
    return [pl.BlockSpec(memory_space=pltpu.VMEM)] * count


IN_HBM = pl.BlockSpec(memory_space=pltpu.HBM)


def call(kernel, name, outs, ins, out_specs, scratch, flops=0):
    return pl.pallas_call(
        kernel,
        in_specs=ins,
        out_specs=out_specs,
        out_shape=[jax.ShapeDtypeStruct(*out) for out in outs],
        scratch_shapes=scratch,
        compiler_params=pltpu.CompilerParams(vmem_limit_bytes=20 * MIB),
        cost_estimate=pl.CostEstimate(flops=flops, bytes_accessed=4 * MIB, transcendentals=0),
        name=name,
    )


def in_hbm(value):
    return pltpu.with_memory_space_constraint(value, pltpu.HBM)


def on_device(cotangent, preact, spectra, spectral_weight, local_weight):
    table = {name: jnp.asarray(value) for name, value in tables().items()}
    swap = [(0, 1), (1, 0)]
    square = (ROWS, HALF)
    turn_scratch = pltpu.VMEM((6 * TILE_Y, TILE_X * QUARTER), BF16)
    cell_scratch = [pltpu.VMEM((CELLS, YS * QUARTER), BF16)] * 2

    slope, send = call(
        slope_kernel,
        "slope",
        [((ROWS, ROW), BF16), (square, F32)],
        [IN_HBM] * 2,
        in_vmem(2),
        [
            pltpu.VMEM((ROWS, ROW), BF16),
            pltpu.VMEM((ROWS, ROW), BF16),
            pltpu.VMEM((ROW, HALF), BF16),
            pltpu.SemaphoreType.DMA((2, CHUNKS)),
        ],
    )(in_hbm(cotangent.reshape(ROWS, ROW)), in_hbm(preact.reshape(ROWS, ROW)))
    depth = lax.ppermute(send, "c", swap)
    own, forward_x, inverse_x, local_map, forward_y, inverse_y = call(
        own_kernel,
        "own_cells",
        [
            ((BLOCK, YS * QUARTER), F32),
            ((2, 2, BLOCK, CELLS), BF16),
            ((2, CELLS, BLOCK), BF16),
            ((16 * CH, 16 * CH), BF16),
            ((2 * KY, 6 * TILE_Y), BF16),
            ((2 * TILE_Y, 6 * KY), BF16),
        ],
        in_vmem(2),
        in_vmem(6),
        [pltpu.VMEM((ROW, HALF), BF16), pltpu.VMEM(square, F32), turn_scratch, *cell_scratch],
        flops=2 * 10**9,
    )(slope, local_weight)
    (partial,) = call(
        modes_kernel,
        "modes",
        [((2048, QUARTER), BF16)],
        in_vmem(4),
        in_vmem(1),
        [turn_scratch, *cell_scratch],
    )(depth, own, forward_x, forward_y)
    partial = lax.all_to_all(partial.reshape(16, 128, QUARTER), PLANE, 0, 0, tiled=True, axis_index_groups=PLANE_ORDER)
    (sums,) = call(
        sum_kernel,
        "sums",
        [((128, QUARTER), BF16)],
        in_vmem(1),
        in_vmem(1),
        [],
    )(partial)
    sums = sums.reshape(32, 4, QUARTER)
    sums = lax.all_to_all(sums, LINE, 0, 0, tiled=True, axis_index_groups=LINE_ORDER)
    grad_weight, back = call(
        update_kernel,
        "update",
        [((2, 8192), F32), ((ZL * ZH, CS, 4, QUARTER), F32)],
        in_vmem(3),
        in_vmem(2),
        [],
    )(
        sums.reshape(ZL * ZH, CS, 4, QUARTER),
        spectra.reshape(2, 2 * HALF),
        spectral_weight.reshape(2, 8192),
    )
    back = lax.all_to_all(
        back.reshape(32, 4, QUARTER).astype(BF16),
        LINE,
        0,
        0,
        tiled=True,
        axis_index_groups=LINE_ORDER,
    )
    back = jnp.broadcast_to(back.reshape(1, 128, QUARTER), (16, 128, QUARTER))
    modes = lax.all_to_all(back, PLANE, 0, 0, tiled=True, axis_index_groups=PLANE_ORDER).reshape(2048, QUARTER)
    other = lax.ppermute(modes, "c", swap)
    back_scratch = [pltpu.VMEM((BLOCK, YS * QUARTER), BF16), turn_scratch]
    (part,) = call(
        expand_own_kernel,
        "expand_own",
        [((ROWS, ROW), F32)],
        in_vmem(6),
        in_vmem(1),
        back_scratch,
        flops=3 * 10**9,
    )(modes, slope, local_map, table["expand"], inverse_x, inverse_y)
    result, grad_weight = call(
        expand_kernel,
        "expand",
        [((ROWS, ROW), F32), ((2, 8192), F32)],
        in_vmem(6),
        [IN_HBM, IN_HBM],
        [
            *back_scratch,
            pltpu.VMEM((ROWS, ROW), F32),
            pltpu.SemaphoreType.DMA((4,)),
            pltpu.SemaphoreType.DMA,
        ],
    )(other, part, table["expand"], inverse_x, inverse_y, grad_weight)
    return result.reshape(TILE_X, TILE_Y, ROW), grad_weight.reshape(1, 2, 8192)


def solution(mesh):
    fine = Mesh(mesh.devices.reshape(ZL, XS, CS, ZH, YS), ("zl", "x", "c", "zh", "y"))
    split_spec = P(("zl", "x", "c"), ("zh", "y"), None)
    return jax.shard_map(
        on_device,
        mesh=fine,
        in_specs=(split_spec, split_spec, split_spec, split_spec, P()),
        out_specs=(split_spec, split_spec),
        check_vma=False,
    )
```
